256 devices in a mesh: lat: 2 (over core), lon: 128 (over z, y, x).
Axes of the slice: x: 4, y: 4, z: 8, core: 2. Of those that a mesh axis runs over, the one named last changes fastest.
Arguments:
- tracer: float32 [4, 5760, 2304], P(None, 'lon', 'lat'), may hold values from -6 to 6
- zonal_wind: float32 [4, 5760, 2304], P(None, 'lon', 'lat'), may hold values from -7.5 to 7.5
- meridional_wind: float32 [4, 5760, 2304], P(None, 'lon', 'lat'), may hold values from -6 to 6
- cutoffs: int32 [2, 384], replicated, may hold values from 1 to 127
Outputs:
- advected: float32 [4, 5760, 2304], P(None, 'lon', 'lat')
The draws below stay inside these ranges and needn't reach their ends.
All inputs are finite; a program needn't handle non-finite values.
Results may differ from the reference program's by a relative error of at most 0.0001.
Values sent between devices are 32-bit elements; how exact they have to be, the bound alone decides.
A program may use at most 64 MiB of HBM per device.

```python
import math
import jax
import jax.numpy as jnp
from jax import lax

LEV = 4
LON = 5760
KMAX = 128
SUBSTEPS = 3
CAP = 384
NLAT = 2304


def zonal_waves(key, amplitude):
    mode_key, phase_key = jax.random.split(key)
    modes = jax.random.randint(mode_key, (LEV, 4), KMAX // 2, 3 * KMAX // 4 + 1)
    phases = jax.random.uniform(phase_key, (LEV, 4), minval=0.0, maxval=2.0 * math.pi)
    columns = jnp.arange(LON, dtype=jnp.int32)
    turns = modes[:, :, None] * columns[None, None, :] % LON
    angles = 2.0 * math.pi / LON * turns.astype(jnp.float32) + phases[:, :, None]
    return amplitude * jnp.sum(jnp.cos(angles), axis=1)


def draw_tracer(key, part):
    key = jax.random.fold_in(key, 11)
    noise_key, wave_key = jax.random.split(key)
    noise = jax.random.normal(noise_key, (LEV, LON, NLAT), dtype=jnp.float32)
    amplitude = 0.75
    waves = zonal_waves(wave_key, amplitude)
    values = noise + waves[:, :, None]
    return jnp.clip(values, -6.0, 6.0).astype(jnp.float32)


def draw_zonal_wind(key, part):
    key = jax.random.fold_in(key, 23)
    sign_key, size_key, noise_key = jax.random.split(key, 3)
    signs = jnp.where(jax.random.bernoulli(sign_key, 0.5, (LEV, 1, 1)), 1.0, -1.0)
    magnitude = jax.random.uniform(size_key, (LEV, 1, 1), minval=3.5, maxval=5.0)
    noise = 0.8 * jax.random.normal(noise_key, (LEV, LON, NLAT), dtype=jnp.float32)
    values = signs * magnitude + noise
    return jnp.clip(values, -7.5, 7.5).astype(jnp.float32)


def with_ends(result, key, low, high):
    shape = result.shape
    index_at = [jax.random.randint(jax.random.fold_in(key, axis), (), 0, shape[axis]) for axis in range(len(shape))]
    result = result.at[tuple(index_at)].set(low)
    longest = shape.index(max(shape))
    index_at[longest] = (index_at[longest] + 1) % shape[longest]
    return result.at[tuple(index_at)].set(high)


def level_of(stream_key, shape, cuts, least, top_value):
    gain, own = 1.0, jax.random.fold_in(stream_key, 6)
    for axis_at, shards_of in cuts:
        heights = jnp.exp(jax.random.uniform(jax.random.fold_in(own, axis_at), (shards_of,), jnp.float32, least / len(cuts), top_value / len(cuts)))
        gain = gain * jnp.repeat(heights, shape[axis_at] // shards_of).reshape([-1 if axis == axis_at else 1 for axis in range(len(shape))])
    return gain


def gaussian(rng, shape, spread, most, cuts=(), kind=jnp.bfloat16):
    array = spread * jax.random.normal(rng, shape, jnp.float32)
    if cuts:
        array = array * level_of(rng, shape, cuts, -0.22, 0.18)
    return jnp.clip(array, -most, most).astype(kind)


def setup_inputs(seed: int = 0) -> dict:
    streams_of = jax.random.split(jax.random.key(seed), 5)
    return {
        "tracer": draw_tracer(jax.random.fold_in(streams_of[4], 71), 0),
        "zonal_wind": draw_zonal_wind(jax.random.fold_in(streams_of[4], 71), 0),
        "meridional_wind": gaussian(streams_of[2], (LEV, LON, NLAT), 1.0, 6.0, ((1, 128), (2, 2)), jnp.float32),
        "cutoffs": with_ends(jax.random.randint(streams_of[3], (2, CAP), 1, KMAX), jax.random.fold_in(streams_of[3], 1), 1, KMAX - 1).astype(jnp.int32),
    }


def fourier_basis(columns, lon_total, mode_count):
    modes = jnp.arange(mode_count, dtype=jnp.int32)
    phase = (columns[:, None] * modes[None, :]) % lon_total
    angles = (2.0 * math.pi / lon_total) * phase.astype(jnp.float32)
    return jnp.concatenate([jnp.cos(angles), jnp.sin(angles)], axis=1)


def mode_weights(lon_total, mode_count):
    modes = jnp.arange(mode_count, dtype=jnp.int32)
    base = jnp.where(modes == 0, 1.0, 2.0).astype(jnp.float32) / lon_total
    return jnp.concatenate([base, base])


def keep_mask(cuts, mode_count):
    modes = jnp.arange(mode_count, dtype=jnp.int32)
    both = jnp.concatenate([modes, modes])
    return (both[None, :] <= cuts[:, None]).astype(jnp.float32)


def apply_filter(flat, cuts, basis_cols, weights):
    coef = jnp.dot(flat, basis_cols, preferred_element_type=jnp.float32, precision=lax.Precision.HIGHEST)
    coef = coef * keep_mask(cuts, KMAX) * weights[None, :]
    return jnp.dot(coef, basis_cols.T, preferred_element_type=jnp.float32, precision=lax.Precision.HIGHEST)


def reference(tracer, zonal_wind, meridional_wind, cutoffs):
    index = jnp.arange(NLAT, dtype=jnp.int32)
    colat = math.pi * (index.astype(jnp.float32) + 0.5) / NLAT
    stretch = (1.0 / jnp.maximum(jnp.sin(colat), 0.125))[None, None, :]
    basis_cols = fourier_basis(jnp.arange(LON, dtype=jnp.int32), LON, KMAX)
    weights = mode_weights(LON, KMAX)
    north_cuts = jnp.broadcast_to(cutoffs[0][None, :], (LEV, CAP)).reshape(-1)
    south_cuts = jnp.broadcast_to(cutoffs[1][None, :], (LEV, CAP)).reshape(-1)
    field = tracer
    for step in range(SUBSTEPS):
        eastern = jnp.roll(field, -1, axis=1)
        western = jnp.roll(field, 1, axis=1)
        top = jnp.roll(field[:, :, 0], LON // 2, axis=1)
        bottom = jnp.roll(field[:, :, -1], LON // 2, axis=1)
        northern = jnp.concatenate([top[:, :, None], field[:, :, :-1]], axis=2)
        southern = jnp.concatenate([field[:, :, 1:], bottom[:, :, None]], axis=2)
        tendency = (-0.05 * stretch * zonal_wind * (eastern - western)
                    - 0.05 * meridional_wind * (northern - southern)
                    + 0.02 * stretch * (eastern - 2.0 * field + western))
        north_flat = jnp.transpose(tendency[:, :, :CAP], (0, 2, 1)).reshape(LEV * CAP, LON)
        south_flat = jnp.transpose(tendency[:, :, NLAT - CAP:], (0, 2, 1)).reshape(LEV * CAP, LON)
        north_new = jnp.transpose(apply_filter(north_flat, north_cuts, basis_cols, weights).reshape(LEV, CAP, LON), (0, 2, 1))
        south_new = jnp.transpose(apply_filter(south_flat, south_cuts, basis_cols, weights).reshape(LEV, CAP, LON), (0, 2, 1))
        tendency = jnp.concatenate([north_new, tendency[:, :, CAP:NLAT - CAP], south_new], axis=2)
        field = field + tendency
    return field
```

```python
import functools
import math

import jax
import jax.numpy as jnp
import numpy as np
from jax import lax
from jax.sharding import PartitionSpec as P

KMAX = 128
CHUNK = 12
WIN = 16
HI = lax.Precision.HIGHEST


def tables(seg, segs):
    total = seg * segs
    k = np.arange(KMAX)
    s = np.arange(segs)
    c = np.arange(seg)
    a = 2 * np.pi * ((k[None, :] * s[:, None]) % segs) / segs
    b = 2 * np.pi * (k[None, :] * c[:, None]) / total
    w = np.where(k == 0, 1.0, 2.0) / total
    f32 = lambda x: np.asarray(x, np.float32)
    return f32(np.cos(a)), f32(np.sin(a)), f32(np.cos(b)), f32(np.sin(b)), f32(w)


def stretch_of(rows, lat_total):
    colat = math.pi * (rows.astype(jnp.float32) + 0.5) / lat_total
    return 1.0 / jnp.maximum(jnp.sin(colat), 0.125)


def tend(mid, east, west, north, south, u, v, s):
    return (
        -0.05 * s * u * (east - west)
        - 0.05 * v * (north - south)
        + 0.02 * s * (east - 2.0 * mid + west)
    )


def body(f, u, v, cutoffs):
    lev, seg, rows = f.shape
    segs = lax.axis_size("lon")
    lat_total = rows * lax.axis_size("lat")
    lat = lax.axis_index("lat")
    lon = lax.axis_index("lon")
    south = lat == 1
    cap = rows // 3
    per = lev * cap // (CHUNK * lev)
    xs = cap + 4
    left = [(i, (i - 1) % segs) for i in range(segs)]
    right = [(i, (i + 1) % segs) for i in range(segs)]
    opposite = [(i, (i + segs // 2) % segs) for i in range(segs)]

    head = jnp.concatenate([f[:, :3], u[:, :2], v[:, :2]], axis=1)
    tail = jnp.concatenate([f[:, -3:], u[:, -2:], v[:, -2:]], axis=1)
    east = lax.ppermute(head, "lon", left)
    west = lax.ppermute(tail, "lon", right)
    edge = lax.ppermute(jnp.where(south, f[:, :, -1], f[:, :, 0]), "lon", opposite)[:, :, None]
    fx = jnp.concatenate([west[:, :3], f, east[:, :3]], axis=1)
    ux = jnp.concatenate([west[:, 3:5], u, east[:, 3:5]], axis=1)
    vx = jnp.concatenate([west[:, 5:], v, east[:, 5:]], axis=1)

    fc = fx[:, 2:-2]
    pad = jnp.pad(edge, ((0, 0), (1, 1), (0, 0)))
    fc = jnp.where(
        south,
        jnp.concatenate([fc[:, :, rows - xs - 1 :], pad], axis=2),
        jnp.concatenate([pad, fc[:, :, : xs + 1]], axis=2),
    )
    cut_rows = lambda a: jnp.where(south, a[:, :, rows - xs :], a[:, :, :xs])
    uc, vc = cut_rows(u), cut_rows(v)
    row0 = jnp.where(south, lat_total - xs, 0)
    sc = stretch_of(row0 + jnp.arange(xs), lat_total)
    t1 = tend(
        fc[:, 1:-1, 1:-1], fc[:, 2:, 1:-1], fc[:, :-2, 1:-1],
        fc[:, 1:-1, :-2], fc[:, 1:-1, 2:], uc, vc, sc,
    )
    sent = jnp.stack([t1, uc, vc], axis=1).transpose(0, 3, 1, 2)
    idx = np.arange(per)[:, None] * CHUNK + np.arange(WIN)[None, :]
    sent = sent[:, idx].reshape(lev * per, WIN, 3, seg)
    got = lax.all_to_all(sent, "lon", 0, 0, tiled=True)
    got = got.transpose(2, 1, 3, 0)
    t1, uw, vw = got[0], got[1], got[2]

    jj = lon % per
    x = jj * CHUNK + jnp.arange(WIN)
    sw = stretch_of(row0 + x, lat_total)[:, None, None]
    in_cap = jnp.where(south, x >= 4, x < cap)
    cut_at = jnp.clip(jnp.where(south, x - 4, x), 0, cap - 1)
    cuts = jnp.where(south, cutoffs[1], cutoffs[0])[cut_at]
    ca, sa, cb, sb, w = tables(seg, segs)
    fwd = np.concatenate([ca, sa], axis=1)
    keep = (jnp.arange(KMAX)[None, :] <= cuts[:, None]) * w[None, :]
    north_pole = (~south) & (jj == 0)
    south_pole = south & (jj == per - 1)

    def filt(t):
        z = jnp.einsum("tcs,sk->tck", t, fwd, precision=HI)
        zc, zs = z[:, :, :KMAX], z[:, :, KMAX:]
        a = jnp.sum(cb * zc - sb * zs, axis=1) * keep
        b = jnp.sum(cb * zs + sb * zc, axis=1) * keep
        a, b = a[:, None], b[:, None]
        d = jnp.concatenate([a * cb + b * sb, b * cb - a * sb], axis=2)
        y = jnp.einsum("tck,sk->tcs", d, fwd, precision=HI)
        return jnp.where(in_cap[:, None, None], y, t)

    def lap(g):
        e = jnp.concatenate([g[:, 1:], jnp.roll(g[:, :1], -1, axis=2)], axis=1)
        ww = jnp.concatenate([jnp.roll(g[:, -1:], 1, axis=2), g[:, :-1]], axis=1)
        half = segs // 2
        first = jnp.where(north_pole, jnp.roll(g[:1], half, axis=2), g[:1])
        last = jnp.where(south_pole, jnp.roll(g[-1:], half, axis=2), g[-1:])
        n = jnp.concatenate([first, g[:-1]], axis=0)
        s = jnp.concatenate([g[1:], last], axis=0)
        return tend(g, e, ww, n, s, uw, vw, sw)

    g = filt(t1)
    g = g + filt(t1 + lap(g))
    g = g + filt(t1 + lap(g))
    back = lax.all_to_all(g.transpose(2, 0, 1), "lon", 0, 0, tiled=True)
    back = back.reshape(lev, per, WIN, seg)
    mid_rows = back[:, :, 2 : 2 + CHUNK].reshape(lev, cap, seg)
    add = jnp.concatenate([back[:, 0, :2], mid_rows, back[:, -1, 14:]], axis=1).transpose(0, 2, 1)

    def edges(a, n):
        return jnp.where(south, a[:, :, :n], a[:, :, rows - n :])

    swap = [(0, 1), (1, 0)]
    halo = lax.ppermute(
        jnp.concatenate([edges(fx, 3), jnp.pad(edges(ux, 2), ((0, 0), (1, 1), (0, 0))), jnp.pad(edges(vx, 2), ((0, 0), (1, 1), (0, 0)))], axis=2),
        "lat", swap,
    )
    fh, uh, vh = halo[:, :, :3], halo[:, 1:-1, 3:5], halo[:, 1:-1, 5:]

    def middle(a, h, extra):
        n = 2 * cap + extra
        return jnp.where(
            south,
            jnp.concatenate([h, a[:, :, :n]], axis=2),
            jnp.concatenate([a[:, :, rows - n :], h], axis=2),
        )

    fm, um, vm = middle(fx, fh, 1), middle(ux, uh, 0), middle(vx, vh, 0)
    first = jnp.where(south, rows - 2, cap)
    sm = stretch_of(first + jnp.arange(2 * cap + 2), lat_total)
    for step in range(3):
        t = tend(
            fm[:, 1:-1, 1:-1], fm[:, 2:, 1:-1], fm[:, :-2, 1:-1],
            fm[:, 1:-1, :-2], fm[:, 1:-1, 2:], um, vm, sm,
        )
        fm = fm[:, 1:-1, 1:-1] + t
        um, vm, sm = um[:, 1:-1, 1:-1], vm[:, 1:-1, 1:-1], sm[1:-1]

    n_out = jnp.concatenate([f[:, :, : cap + 2] + add[:, :, : cap + 2], fm], axis=2)
    s_out = jnp.concatenate([fm, f[:, :, rows - cap - 2 :] + add[:, :, 2:]], axis=2)
    return jnp.where(south, s_out, n_out)


def solution(mesh):
    placed = (P(None, "lon", "lat"), P(None, "lon", "lat"), P(None, "lon", "lat"), P())
    return jax.shard_map(
        body, mesh=mesh, in_specs=placed, out_specs=P(None, "lon", "lat"), check_vma=False
    )
```

```python
import functools
import math

import jax
import jax.numpy as jnp
import ml_dtypes
import numpy as np
from jax import lax
from jax.experimental import pallas as pl
from jax.experimental.pallas import tpu as pltpu
from jax.sharding import PartitionSpec as P

MESH = pl.DeviceIdType.MESH
LEV, SEG, ROWS, SEGS = 4, 45, 1152, 128
CAP = ROWS // 3
CHUNK, WIN = 12, 16
PER = CAP // CHUNK
CW = 512
SHIFT = CW - CAP - 4
MW = 1024
KMAX = 128
C8 = 48
TAIL = 7
F32, BF16 = jnp.float32, jnp.bfloat16


def split(x):
    hi = x.astype(ml_dtypes.bfloat16)
    return hi, (x - hi.astype(np.float32)).astype(ml_dtypes.bfloat16)


def tables():
    total = SEG * SEGS
    k, s, c = np.arange(KMAX), np.arange(SEGS), np.arange(SEG)
    a = 2 * np.pi * ((s[:, None] * k[None, :]) % SEGS) / SEGS
    b = 2 * np.pi * (c[:, None] * k[None, :]) / total
    fwd = np.concatenate([np.cos(a), np.sin(a)], axis=1).astype(np.float32)
    pad = ((0, C8 - SEG), (0, 0))
    cb = np.pad(np.cos(b), pad).astype(np.float32)
    sb = np.pad(np.sin(b), pad).astype(np.float32)
    w = (np.where(k == 0, 1.0, 2.0) / total).astype(np.float32)[None, :]
    return split(fwd) + split(np.ascontiguousarray(fwd.T)) + (cb, sb, w)


def stretch_table():
    colat = np.float32(math.pi) * (np.arange(2 * ROWS).astype(np.float32) + np.float32(0.5))
    colat = (colat / np.float32(2 * ROWS)).astype(np.float32)
    s = np.float32(1.0) / np.maximum(np.sin(colat), np.float32(0.125))
    s = np.pad(s.astype(np.float32), (0, MW))
    cap = np.stack([s[:CW], s[2 * ROWS - CW : 2 * ROWS]])[:, None, :]
    mid = np.stack([s[256 : 256 + MW], s[ROWS - 128 : ROWS - 128 + MW]])[:, None, :]
    rows = np.stack([s[: CAP + 4], s[2 * ROWS - CAP - 4 : 2 * ROWS]])
    return cap, mid, rows


def tend(mid, east, west, north, south, u, v, s):
    return (
        -0.05 * s * u * (east - west)
        - 0.05 * v * (north - south)
        + 0.02 * s * (east - 2.0 * mid + west)
    )


def dot3(x, hi_ref, lo_ref):
    hi = x.astype(BF16)
    lo = (x - hi.astype(F32)).astype(BF16)
    dot = functools.partial(jnp.dot, preferred_element_type=F32)
    return dot(hi, hi_ref[...]) + (dot(lo, hi_ref[...]) + dot(hi, lo_ref[...]))


def kernel(
    f, u, v, cuts, rows_s, cap_s, mid_s, fh, fl, ih, il, cb_ref, sb_ref, w_ref,
    out,
    edge_w, edge_e, edge_o, got_w, got_e, got_o, mid_w, mid_e, mgot_w, mgot_e,
    fm, um, vm, fb, mm, mx, ln, lx, msg, recv, ext, ext_got, sp,
    tt, uu, vv, gg, xt, zz, dd, sb128, ret, back, rl,
    hs, hr, ms, mr, ls, lr, a_s, a_r, x_s, x_r, b_s, b_r,
):
    lat = lax.axis_index("lat")
    lon = lax.axis_index("lon")
    south = lat == 1
    jj = lax.rem(lon, PER)
    north_pole = jnp.logical_and(lat == 0, jj == 0)
    south_pole = jnp.logical_and(lat == 1, jj == PER - 1)
    at = lambda d: (lat, d)
    east_dev = at(lax.rem(lon + 1, SEGS))
    west_dev = at(lax.rem(lon + SEGS - 1, SEGS))
    opp_dev = at(lax.rem(lon + SEGS // 2, SEGS))
    partner = (1 - lat, lon)

    barrier = pltpu.get_barrier_semaphore()

    @pl.loop(1, SEGS)
    def _(k):
        pl.semaphore_signal(barrier, inc=1, device_id=at(lax.rem(lon + k, SEGS)), device_id_type=MESH)

    pl.semaphore_signal(barrier, inc=1, device_id=partner, device_id_type=MESH)

    cap0 = pl.multiple_of(lat * (ROWS - CW), 128)
    mid0 = pl.multiple_of((1 - lat) * 256, 128)
    edge0 = pl.multiple_of(lat * (ROWS - 128), 128)
    lane = lax.broadcasted_iota(jnp.int32, (C8, 128), 1)

    edge_o[...] = jnp.zeros_like(edge_o)
    edge_w[...] = jnp.zeros_like(edge_w)
    edge_e[...] = jnp.zeros_like(edge_e)
    mid_w[...] = jnp.zeros_like(mid_w)
    mid_e[...] = jnp.zeros_like(mid_e)
    for l in range(LEV):
        edge_w[l : l + 1] = f[l, 0:1, pl.ds(cap0, CW)]
        edge_e[l : l + 1] = f[l, SEG - 1 : SEG, pl.ds(cap0, CW)]
        tile = pltpu.roll(f[l, :, pl.ds(edge0, 128)], l + lat, 1)
        edge_o[0:SEG] = jnp.where(lane[:SEG] == l, tile, edge_o[0:SEG])
        for a, ref, n in ((0, f, 3), (3, u, 2), (5, v, 2)):
            mid_w[l, a : a + n] = ref[l, 0:n, pl.ds(mid0, MW - 128)]
            mid_e[l, a : a + n] = ref[l, SEG - n : SEG, pl.ds(mid0, MW - 128)]

    pl.semaphore_wait(barrier, SEGS)

    def remote(src, dst, send, recv_sem, dev):
        return pltpu.make_async_remote_copy(
            src_ref=src, dst_ref=dst, send_sem=send, recv_sem=recv_sem,
            device_id=dev, device_id_type=MESH,
        )

    halos = [
        remote(edge_w, got_e, hs.at[0], hr.at[0], west_dev),
        remote(edge_e, got_w, hs.at[1], hr.at[1], east_dev),
        remote(edge_o, got_o, hs.at[2], hr.at[2], opp_dev),
    ]
    mids = [
        remote(mid_w, mgot_e, ms.at[0], mr.at[0], west_dev),
        remote(mid_e, mgot_w, ms.at[1], mr.at[1], east_dev),
    ]
    for c in halos:
        c.start()
    for c in mids:
        c.start()
    for c in halos:
        c.wait()

    lanes = lax.broadcasted_iota(jnp.int32, (C8, CW), 1)
    scap = cap_s[lat]

    @pl.loop(0, LEV)
    def _(l):
        fb[8 : 8 + SEG] = f[l, :, pl.ds(cap0, CW)]
        fb[7:8] = got_w[pl.ds(l, 1)]
        fb[8 + SEG : 9 + SEG] = got_e[pl.ds(l, 1)]
        mid = fb[8 : 8 + C8]
        o = pltpu.roll(got_o[...], lax.rem(lat * 127 - l + 128, 128), 1)
        o = jnp.concatenate([o, o, o, o], axis=1)
        n = jnp.where(jnp.logical_and(lanes == 0, lat == 0), o, pltpu.roll(mid, 1, 1))
        s = jnp.where(jnp.logical_and(lanes == CW - 1, lat == 1), o, pltpu.roll(mid, CW - 1, 1))
        uc = u[l, :, pl.ds(cap0, CW)]
        vc = v[l, :, pl.ds(cap0, CW)]
        t1 = tend(mid[:SEG], fb[9 : 9 + SEG], fb[7 : 7 + SEG], n[:SEG], s[:SEG], uc, vc, scap)
        turn = lax.rem(CW - lat * SHIFT, CW)
        mm[0:SEG] = pltpu.roll(t1, turn, 1)
        mm[SEG : 2 * SEG] = pltpu.roll(uc, turn, 1)
        mm[2 * SEG : 3 * SEG] = pltpu.roll(vc, turn, 1)
        vt = mm[128 : 128 + TAIL]
        x12 = lax.rem(lanes[:TAIL], 12)
        mx[...] = mm[0:128]
        for i in range(8):
            t0 = i + 1 if i < 7 else 15
            t15 = i + 8 if i < 7 else 0
            a0 = pltpu.roll(vt, CW - t0, 1)
            a15 = pltpu.roll(vt, 15 - t15, 1)
            mx[SEG + TAIL * i : SEG + TAIL * (i + 1)] = jnp.where(x12 == 3, a15, a0)
        for b in range(CW // 128):
            ln[128 * b : 128 * (b + 1)] = mm[0:128, 128 * b : 128 * (b + 1)].T
            lx[128 * b : 128 * (b + 1)] = mx[0:128, 128 * b : 128 * (b + 1)].T
        row = lax.broadcasted_iota(jnp.int32, (WIN, 128), 0)

        @pl.loop(0, PER // 2)
        def _(m):
            a = ln[pl.ds(pl.multiple_of(24 * m, 8), 32)]
            b = lx[pl.ds(pl.multiple_of(24 * m, 8), 32)]
            first = jnp.logical_and(m == 0, lat == 0)
            last = jnp.logical_and(m == PER // 2 - 1, lat == 1)
            use0 = jnp.logical_or(jnp.logical_and(row == 0, jnp.logical_not(first)), row == WIN - 1)
            use1 = jnp.logical_or(row == 0, jnp.logical_and(row == WIN - 1, jnp.logical_not(last)))
            msg[l * PER + 2 * m] = jnp.where(use0, b[0:16], a[0:16])
            msg[l * PER + 2 * m + 1] = jnp.where(use1, b[12:28], a[12:28])

        ext[l] = jnp.where(lat == 0, lx[0:8], lx[PER * CHUNK - CHUNK + 8 : PER * CHUNK - CHUNK + 16])

    recv[lon] = msg[lon]

    def send_line(d):
        return remote(msg.at[d], recv.at[lon], a_s, a_r, at(d))

    @pl.loop(1, SEGS // 2)
    def _(k):
        send_line(lax.rem(lon + k, SEGS)).start()
        send_line(lax.rem(lon + SEGS - k, SEGS)).start()

    send_line(lax.rem(lon + SEGS // 2, SEGS)).start()

    def send_ext(l):
        d = l * PER + lat * (PER - 1)
        return d, remote(ext.at[l], ext_got.at[lon], x_s.at[l], x_r, at(d))

    for l in range(LEV):
        d, c = send_ext(l)

        @pl.when(d != lon)
        def _():
            c.start()

        @pl.when(d == lon)
        def _():
            ext_got[lon] = ext[l]

    for c in mids:
        c.wait()
    own = pl.multiple_of(lat * 128, 128)

    @pl.loop(0, LEV)
    def _(l):
        for ref, src, a, n in ((fm, f, 0, 3), (um, u, 3, 2), (vm, v, 5, 2)):
            ref[l, 3 : 3 + SEG, pl.ds(own, MW - 128)] = src[l, :, pl.ds(mid0, MW - 128)]
            ref[l, 3 - n : 3, pl.ds(own, MW - 128)] = mgot_w[l, a : a + n]
            ref[l, 3 + SEG : 3 + SEG + n, pl.ds(own, MW - 128)] = mgot_e[l, a : a + n]

    src0 = pl.multiple_of((1 - lat) * (MW - 256) + lat * 128, 128)
    dst0 = pl.multiple_of(lat * (MW - 128), 128)
    lats = [
        remote(ref.at[:, :, pl.ds(src0, 128)], ref.at[:, :, pl.ds((1 - lat) * 0 + dst0, 128)], ls.at[i], lr.at[i], partner)
        for i, ref in enumerate((fm, um, vm))
    ]
    for c in lats:
        c.start()
    for c in lats:
        c.wait()
    smid = mid_s[lat]

    @pl.loop(0, LEV)
    def _(l):
        for _ in range(3):
            x = fm[l]
            t = tend(
                x, pltpu.roll(x, 55, 0), pltpu.roll(x, 1, 0),
                pltpu.roll(x, 1, 1), pltpu.roll(x, MW - 1, 1), um[l], vm[l], smid,
            )
            fm[l] = x + t

    def total(sem, ref, n):
        pltpu.make_async_copy(ref.at[pl.ds(0, n)], ref.at[pl.ds(0, n)], sem).wait()

    total(a_r, recv, SEGS - 1)
    tt[:, SEG:C8] = jnp.zeros((WIN, C8 - SEG, 128), F32)
    uu[:, SEG:C8] = jnp.zeros((WIN, C8 - SEG, 128), F32)
    vv[:, SEG:C8] = jnp.zeros((WIN, C8 - SEG, 128), F32)
    for t in range(WIN):
        w = recv[:, t, :].T
        tt[t, 0:SEG] = w[0:SEG]
        uu[t, 0:SEG] = w[SEG : 2 * SEG]
        vv[t, 0 : SEG - TAIL] = w[2 * SEG : 128]
        if t == 0:
            sp[0] = w
        if t == WIN - 1:
            sp[1] = w

    @pl.when(jnp.logical_or(north_pole, south_pole))
    def _():
        total(x_r, ext_got, SEGS - 1)

    @pl.when(north_pole)
    def _():
        sp[0] = ext_got[:, 0, :].T

    @pl.when(south_pole)
    def _():
        sp[1] = ext_got[:, 7, :].T

    for i in range(8):
        t0 = i + 1 if i < 7 else 15
        t15 = i + 8 if i < 7 else 0
        lo, hi = SEG + TAIL * i, SEG + TAIL * (i + 1)
        vv[t0, SEG - TAIL : SEG] = sp[0, lo:hi]
        vv[t15, SEG - TAIL : SEG] = sp[1, lo:hi]

    col = lax.broadcasted_iota(jnp.int32, (C8, 128), 0)
    k_lane = lax.broadcasted_iota(jnp.int32, (1, KMAX), 1)
    cb, sb = cb_ref[...], sb_ref[...]

    for step in range(3):
        if step == 0:
            x_all = tt[...]
        else:

            @pl.loop(0, WIN)
            def _(t):
                g = gg[t]
                g8 = pltpu.roll(g[0:8], 127, 1)
                g40 = pltpu.roll(g[40:48], 1, 1)
                e = jnp.where(col == SEG - 1, jnp.broadcast_to(g8[0:1], (C8, 128)), pltpu.roll(g, C8 - 1, 0))
                w = jnp.where(col == 0, jnp.broadcast_to(g40[4:5], (C8, 128)), pltpu.roll(g, 1, 0))
                flip = pltpu.roll(g, SEGS // 2, 1)
                n = jnp.where(jnp.logical_and(north_pole, t == 0), flip, gg[jnp.maximum(t - 1, 0)])
                s = jnp.where(jnp.logical_and(south_pole, t == WIN - 1), flip, gg[jnp.minimum(t + 1, WIN - 1)])
                sw = rows_s[lat, CHUNK * jj + t]
                xt[t] = tt[t] + tend(g, e, w, n, s, uu[t], vv[t], sw)

            x_all = xt[...]
        x_all = x_all.reshape(WIN * C8, 128)
        zz[...] = dot3(x_all, fh, fl).reshape(WIN, C8, 2 * KMAX)

        @pl.loop(0, WIN)
        def _(t):
            zc, zs = zz[t, :, 0:KMAX], zz[t, :, KMAX:]
            x = CHUNK * jj + t - 4 * lat
            cut = cuts[lat, jnp.minimum(jnp.maximum(x, 0), CAP - 1)]
            keep = jnp.where(k_lane <= cut, w_ref[...], 0.0)
            a = jnp.sum(cb * zc - sb * zs, axis=0, keepdims=True) * keep
            b = jnp.sum(cb * zs + sb * zc, axis=0, keepdims=True) * keep
            dd[t, :, 0:KMAX] = a * cb + b * sb
            dd[t, :, KMAX:] = b * cb - a * sb

        zz[:, :, 0:128] = dot3(dd[...].reshape(WIN * C8, 2 * KMAX), ih, il).reshape(WIN, C8, 128)

        @pl.loop(0, WIN)
        def _(t):
            x = CHUNK * jj + t - 4 * lat
            inside = jnp.logical_and(x >= 0, x < CAP)
            raw = tt[t] if step == 0 else xt[t]
            y = jnp.where(inside, zz[t, :, 0:128], raw)
            gg[t] = y if step == 0 else gg[t] + y

    sb128[...] = jnp.zeros_like(sb128)
    for p in range(8):
        tb = 10 + p if p < 4 else (0, 1, 14, 15)[p - 4]
        sb128[0:C8] = gg[2 + p]
        sb128[64 : 64 + C8] = gg[tb]
        ret[:, p, :] = sb128[...].T

    back[lon] = ret[lon]

    def send_back(d):
        return remote(ret.at[d], back.at[lon], b_s, b_r, at(d))

    @pl.loop(1, SEGS // 2)
    def _(k):
        send_back(lax.rem(lon + k, SEGS)).start()
        send_back(lax.rem(lon + SEGS - k, SEGS)).start()

    send_back(lax.rem(lon + SEGS // 2, SEGS)).start()

    @pl.loop(0, LEV)
    def _(l):
        out[l, :, pl.ds(mid0, MW - 128)] = fm[l, 3 : 3 + SEG, pl.ds(own, MW - 128)]

    total(b_r, back, SEGS - 1)
    row8 = lax.broadcasted_iota(jnp.int32, (8, 128), 0)

    @pl.loop(0, LEV)
    def _(l):
        rl[CAP:CW] = jnp.zeros((CW - CAP, 128), F32)

        @pl.loop(0, PER // 2)
        def _(m):
            a0, a1 = back[l * PER + 2 * m], back[l * PER + 2 * m + 1]
            b0, b1 = pltpu.roll(a0, 64, 1), pltpu.roll(a1, 64, 1)
            a1r = pltpu.roll(a1, 4, 0)
            base = pl.multiple_of(24 * m + 8, 8)
            rl[pl.ds(base, 8)] = a0
            rl[pl.ds(pl.multiple_of(base + 8, 8), 8)] = jnp.where(row8 < 4, b0, a1r)
            rl[pl.ds(pl.multiple_of(base + 16, 8), 8)] = jnp.where(row8 < 4, a1r, pltpu.roll(b1, 4, 0))

        rl[0:8] = pltpu.roll(pltpu.roll(back[l * PER], 64, 1), 2, 0)
        rl[CAP + 8 : CAP + 16] = pltpu.roll(pltpu.roll(back[l * PER + PER - 1], 64, 1), 2, 0)
        add = jnp.concatenate([rl[128 * b : 128 * (b + 1)].T[0:C8] for b in range(CW // 128)], axis=1)
        add = pltpu.roll(add, lax.rem(lat * SHIFT + CW - 6, CW), 1)[0:SEG]
        x = lanes[:SEG] - lat * SHIFT
        inside = jnp.logical_and(x >= 2 * lat, x < CAP + 2 + 2 * lat)
        old = out[l, :, pl.ds(cap0, CW)]
        out[l, :, pl.ds(cap0, CW)] = jnp.where(inside, f[l, :, pl.ds(cap0, CW)] + add, old)

    total(a_s, msg, SEGS - 1)
    total(b_s, ret, SEGS - 1)
    for l in range(LEV):
        d, c = send_ext(l)

        @pl.when(d != lon)
        def _():
            c.wait_send()


def body(f, u, v, cutoffs):
    cap_s, mid_s, rows_s = stretch_table()
    vmem = pl.BlockSpec(memory_space=pltpu.VMEM)
    smem = pl.BlockSpec(memory_space=pltpu.SMEM)
    V = lambda *shape: pltpu.VMEM(shape, F32)
    dma = pltpu.SemaphoreType.DMA
    return pl.pallas_call(
        kernel,
        out_shape=jax.ShapeDtypeStruct(f.shape, F32),
        in_specs=[vmem] * 3 + [smem] * 2 + [vmem] * 9,
        out_specs=vmem,
        scratch_shapes=[
            V(8, CW), V(8, CW), V(C8, 128), V(8, CW), V(8, CW), V(C8, 128),
            V(LEV, 8, MW - 128), V(LEV, 8, MW - 128), V(LEV, 8, MW - 128), V(LEV, 8, MW - 128),
            V(LEV, 56, MW), V(LEV, 56, MW), V(LEV, 56, MW),
            V(64, CW), V(136, CW), V(128, CW), V(CW, 128), V(CW, 128),
            V(SEGS, WIN, 128), V(SEGS, WIN, 128), V(LEV, 8, 128), V(SEGS, 8, 128), V(2, 128, 128),
            V(WIN, C8, 128), V(WIN, C8, 128), V(WIN, C8, 128), V(WIN, C8, 128), V(WIN, C8, 128),
            V(WIN, C8, 256), V(WIN, C8, 256), V(128, 128), V(SEGS, 8, 128), V(SEGS, 8, 128), V(CW, 128),
            dma((3,)), dma((3,)), dma((2,)), dma((2,)), dma((3,)), dma((3,)),
            dma, dma, dma((LEV,)), dma, dma, dma,
        ],
        compiler_params=pltpu.CompilerParams(
            collective_id=0, has_side_effects=True, vmem_limit_bytes=40 * 1024 * 1024
        ),
    )(f, u, v, cutoffs, rows_s, cap_s, mid_s, *tables())


def solution(mesh):
    placed = (P(None, "lon", "lat"), P(None, "lon", "lat"), P(None, "lon", "lat"), P())
    return jax.shard_map(
        body, mesh=mesh, in_specs=placed, out_specs=P(None, "lon", "lat"), check_vma=False
    )
```

```python
import functools
import math

import jax
import jax.numpy as jnp
import ml_dtypes
import numpy as np
from jax import lax
from jax.experimental import pallas as pl
from jax.experimental.pallas import tpu as pltpu
from jax.sharding import PartitionSpec as P

MESH = pl.DeviceIdType.MESH
LEV, SEG, ROWS, SEGS = 4, 45, 1152, 128
CAP = ROWS // 3
CHUNK, WIN = 12, 16
PER = CAP // CHUNK
CW = 512
SHIFT = CW - CAP - 4
MW = 1024
KMAX = 128
C8 = 48
RET = 5
COLS = 101
TAIL = 7
F32, BF16 = jnp.float32, jnp.bfloat16


def split(x):
    hi = x.astype(ml_dtypes.bfloat16)
    return hi, (x - hi.astype(np.float32)).astype(ml_dtypes.bfloat16)


def two_parts(basis):
    hi, lo = split(np.ascontiguousarray(basis))
    return np.concatenate(
        [np.concatenate([hi, lo], axis=1), np.concatenate([hi, np.zeros_like(lo)], axis=1)], axis=0
    )


def tables():
    total = SEG * SEGS
    half = KMAX // 2
    m, s, c = np.arange(half), np.arange(SEGS), np.arange(SEG)
    a = 2 * np.pi * ((s[:, None] * m[None, :]) % SEGS) / SEGS
    sin = np.sin(a)
    sin[:, 0] = np.where(s % 2 == 0, 1.0, -1.0)
    basis = np.concatenate([np.cos(a), sin], axis=1).astype(np.float32)
    other = np.where(m == 0, half, KMAX - m)
    angle = lambda k: 2 * np.pi * (c[:, None] * k[None, :]) / total
    cm, sm, co, so = np.cos(angle(m)), np.sin(angle(m)), np.cos(angle(other)), np.sin(angle(other))
    ta, tb = np.concatenate([cm, -sm], axis=1), np.concatenate([sm, cm], axis=1)
    pa, pb = np.concatenate([co, so], axis=1), np.concatenate([so, -co], axis=1)
    ta[:, half], tb[:, half], pa[:, 0], pb[:, 0] = 0.0, 0.0, 0.0, 0.0
    pa[:, half], pb[:, half] = co[:, 0], so[:, 0]
    twiddle = np.pad(np.stack([ta, tb, pa, pb]), ((0, 0), (0, C8 - SEG), (0, 0))).astype(np.float32)
    return two_parts(basis), two_parts(basis.T), twiddle


def stretch_table():
    colat = np.float32(math.pi) * (np.arange(2 * ROWS).astype(np.float32) + np.float32(0.5))
    colat = (colat / np.float32(2 * ROWS)).astype(np.float32)
    s = np.float32(1.0) / np.maximum(np.sin(colat), np.float32(0.125))
    s = np.pad(s.astype(np.float32), (0, MW))
    cap = np.stack([s[:CW], s[2 * ROWS - CW : 2 * ROWS]])[:, None, :]
    mid = np.stack([s[256 : 256 + MW], s[ROWS - 128 : ROWS - 128 + MW]])[:, None, :]
    rows = np.stack([s[: CAP + 4], s[2 * ROWS - CAP - 4 : 2 * ROWS]])
    return cap, mid, rows


def tend(mid, east, west, north, south, u, v, s):
    return (
        -0.05 * s * u * (east - west)
        - 0.05 * v * (north - south)
        + 0.02 * s * (east - 2.0 * mid + west)
    )


def product(x, parts_ref):
    hi = x.astype(BF16)
    lo = (x - hi.astype(F32)).astype(BF16)
    r = jnp.dot(jnp.concatenate([hi, lo], axis=1), parts_ref[...], preferred_element_type=F32)
    return r[:, 0:128] + r[:, 128:]


def kernel(
    f_hbm, u_hbm, v_hbm, cuts, rows_s, cap_s, mid_s, fwd, inv, twiddle,
    out,
    f, u, v, mid_w, mid_e, mgot_w, mgot_e,
    fm, um, vm, mm, mx, ln, lx, msg, recv, ext, ext_got, sp,
    tt, uu, vv, ga, gb, st, ret, back, rl,
    cs, os, ms, mr, ls, lr, a_s, a_r, x_s, x_r, b_s, b_r,
):
    lat = lax.axis_index("lat")
    lon = lax.axis_index("lon")
    south = lat == 1
    jj = lax.rem(lon, PER)
    north_pole = jnp.logical_and(lat == 0, jj == 0)
    south_pole = jnp.logical_and(lat == 1, jj == PER - 1)
    at = lambda d: (lat, d)
    east_dev = at(lax.rem(lon + 1, SEGS))
    west_dev = at(lax.rem(lon + SEGS - 1, SEGS))
    partner = (1 - lat, lon)

    cap0 = pl.multiple_of(lat * (ROWS - CW), 128)
    mid0 = pl.multiple_of((1 - lat) * 256, 128)
    rest0 = pl.multiple_of((1 - lat) * CW, 128)
    pairs = ((f_hbm, f), (u_hbm, u), (v_hbm, v))

    caps = [
        pltpu.make_async_copy(src.at[:, :, pl.ds(cap0, CW)], dst.at[:, :, pl.ds(cap0, CW)], cs.at[i])
        for i, (src, dst) in enumerate(pairs)
    ]
    others = [
        pltpu.make_async_copy(
            src.at[:, :, pl.ds(rest0, ROWS - CW)], dst.at[:, :, pl.ds(rest0, ROWS - CW)], os.at[i]
        )
        for i, (src, dst) in enumerate(pairs)
    ]
    for c in caps:
        c.start()

    barrier = pltpu.get_barrier_semaphore()

    def greet(k):
        pl.semaphore_signal(barrier, inc=1, device_id=at(lax.rem(lon + k, SEGS)), device_id_type=MESH)

    @pl.loop(0, (SEGS - 1) // 8)
    def _(k):
        for i in range(8):
            greet(8 * k + i + 1)

    for k in range((SEGS - 1) // 8 * 8 + 1, SEGS):
        greet(k)
    pl.semaphore_signal(barrier, inc=1, device_id=partner, device_id_type=MESH)

    for c in others:
        c.start()

    lanes = lax.broadcasted_iota(jnp.int32, (C8, CW), 1)
    scap = cap_s[lat]
    row = lax.broadcasted_iota(jnp.int32, (WIN, 128), 0)
    lane1 = lanes[:SEG]
    pole = jnp.where(lat == 0, 0, CW - 1)

    for c in caps:
        c.wait()

    @pl.loop(0, LEV)
    def _(l):
        fc = f[l, :, pl.ds(cap0, CW)]
        uc = u[l, :, pl.ds(cap0, CW)]
        vc = v[l, :, pl.ds(cap0, CW)]
        zero = jnp.zeros((1, CW), F32)
        e = jnp.concatenate([fc[1:], zero], axis=0)
        w = jnp.concatenate([zero, fc[:-1]], axis=0)
        n = jnp.where(jnp.logical_and(lane1 == pole, lat == 0), 0.0, pltpu.roll(fc, 1, 1))
        s = jnp.where(jnp.logical_and(lane1 == pole, lat == 1), 0.0, pltpu.roll(fc, CW - 1, 1))
        turn = lax.rem(CW - lat * SHIFT, CW)
        mm[0:SEG] = pltpu.roll(tend(fc, e, w, n, s, uc, vc, scap), turn, 1)
        mm[SEG : 2 * SEG] = pltpu.roll(uc, turn, 1)
        mm[2 * SEG : 3 * SEG] = pltpu.roll(vc, turn, 1)
        vt = mm[128 : 128 + TAIL]
        x12 = lax.rem(lanes[:WIN], 12)
        edge = pltpu.roll(fc, lax.rem(CW - lat * (SHIFT + 2) + 1, CW), 1)
        mx[0:SEG] = jnp.where(lane1 == jnp.where(lat == 0, 1, CAP + 2), edge, mm[0:SEG])
        for i in range(8):
            t0 = i + 1 if i < 7 else 15
            t15 = i + 8 if i < 7 else 0
            a0 = pltpu.roll(vt, CW - t0, 1)
            a15 = pltpu.roll(vt, 15 - t15, 1)
            mx[SEG + TAIL * i : SEG + TAIL * (i + 1)] = jnp.where(x12[:TAIL] == 3, a15, a0)
        ft = pltpu.roll(fc, turn, 1)
        f0 = jnp.broadcast_to(ft[0:1], (WIN, CW))
        f44 = jnp.broadcast_to(ft[SEG - 1 : SEG], (WIN, CW))
        f0 = pltpu.roll(f0, CW - 15, 1, stride=1, stride_axis=0)
        f44 = pltpu.roll(f44, 0, 1, stride=1, stride_axis=0)
        mx[COLS : COLS + WIN] = jnp.where(x12 == 3, f44, f0)
        mx[COLS + WIN : COLS + WIN + 1] = mm[SEG : SEG + 1]
        mx[COLS + WIN + 1 : COLS + WIN + 2] = mm[2 * SEG - 1 : 2 * SEG]
        for b in range(CW // 128):
            ln[128 * b : 128 * (b + 1)] = mm[0:128, 128 * b : 128 * (b + 1)].T
            lx[128 * b : 128 * (b + 1)] = mx[0:128, 128 * b : 128 * (b + 1)].T

        @pl.loop(0, PER // 8)
        def _(mo):
            for mi in range(4):
                m = 4 * mo + mi
                a = ln[pl.ds(pl.multiple_of(24 * m, 8), 32)]
                b = lx[pl.ds(pl.multiple_of(24 * m, 8), 32)]
                first = jnp.logical_and(m == 0, lat == 0)
                last = jnp.logical_and(m == PER // 2 - 1, lat == 1)
                use0 = jnp.logical_or(jnp.logical_and(row == 0, jnp.logical_not(first)), row == WIN - 1)
                use1 = jnp.logical_or(row == 0, jnp.logical_and(row == WIN - 1, jnp.logical_not(last)))
                msg[l * PER + 2 * m] = jnp.where(use0, b[0:16], a[0:16])
                msg[l * PER + 2 * m + 1] = jnp.where(use1, b[12:28], a[12:28])

        ext[l] = jnp.where(lat == 0, lx[0:8], lx[CAP - 4 : CAP + 4])

    pl.semaphore_wait(barrier, SEGS)

    def remote(src, dst, send, recv_sem, dev):
        return pltpu.make_async_remote_copy(
            src_ref=src, dst_ref=dst, send_sem=send, recv_sem=recv_sem,
            device_id=dev, device_id_type=MESH,
        )

    def send_line(d):
        return remote(msg.at[d], recv.at[lon], a_s, a_r, at(d))

    def spread(send):
        @pl.loop(0, (SEGS // 2 - 1) // 7)
        def _(k):
            for i in range(1, 8):
                send(lax.rem(lon + 7 * k + i, SEGS)).start()
                send(lax.rem(lon + SEGS - 7 * k - i, SEGS)).start()

        send(lax.rem(lon + SEGS // 2, SEGS)).start()

    spread(send_line)
    recv[lon] = msg[lon]

    def send_ext(l):
        d = l * PER + lat * (PER - 1)
        return d, remote(ext.at[l], ext_got.at[lon], x_s.at[l], x_r, at(d))

    for l in range(LEV):
        d, c = send_ext(l)

        @pl.when(d != lon)
        def _():
            c.start()

        @pl.when(d == lon)
        def _():
            ext_got[lon] = ext[l]

    for c in others:
        c.wait()
    own = pl.multiple_of(lat * 128, 128)
    mid_w[...] = jnp.zeros_like(mid_w)
    mid_e[...] = jnp.zeros_like(mid_e)
    parts = ((fm, f, 0, 3), (um, u, 3, 2), (vm, v, 5, 2))
    for l in range(LEV):
        for ref, src, a, n in parts:
            mid_w[l, a : a + n] = src[l, 0:n, pl.ds(mid0, MW - 128)]
            mid_e[l, a : a + n] = src[l, SEG - n : SEG, pl.ds(mid0, MW - 128)]

    @pl.loop(0, LEV)
    def _(l):
        for ref, src, a, n in parts:
            ref[l, 3 : 3 + SEG, pl.ds(own, MW - 128)] = src[l, :, pl.ds(mid0, MW - 128)]

    mids = [
        remote(mid_w, mgot_e, ms.at[0], mr.at[0], west_dev),
        remote(mid_e, mgot_w, ms.at[1], mr.at[1], east_dev),
    ]
    src0 = pl.multiple_of((1 - lat) * (MW - 256) + lat * 128, 128)
    dst0 = pl.multiple_of(lat * (MW - 128), 128)
    lats = [
        remote(ref.at[:, :, pl.ds(src0, 128)], ref.at[:, :, pl.ds(dst0, 128)], ls.at[i], lr.at[i], partner)
        for i, ref in enumerate((fm, um, vm))
    ]

    def total(sem, ref, n):
        pltpu.make_async_copy(ref.at[pl.ds(0, n)], ref.at[pl.ds(0, n)], sem).wait()

    total(a_r, recv, SEGS - 1)
    for c in mids:
        c.start()
    tt[:, SEG:C8] = jnp.zeros((WIN, C8 - SEG, 128), F32)
    uu[:, SEG:C8] = jnp.zeros((WIN, C8 - SEG, 128), F32)
    vv[:, SEG:C8] = jnp.zeros((WIN, C8 - SEG, 128), F32)
    for t in range(WIN):
        w = recv[:, t, :].T
        tt[t, 0:SEG] = w[0:SEG]
        uu[t, 0:SEG] = w[SEG : 2 * SEG]
        vv[t, 0 : SEG - TAIL] = w[2 * SEG : 128]
        if t == 0:
            sp[0] = w
        if t == WIN - 1:
            sp[1] = w

    @pl.when(jnp.logical_or(north_pole, south_pole))
    def _():
        total(x_r, ext_got, SEGS - 1)

    sp[2] = jnp.zeros((128, 128), F32)

    @pl.when(north_pole)
    def _():
        sp[0] = ext_got[:, 0, :].T
        sp[2] = ext_got[:, 1, :].T

    @pl.when(south_pole)
    def _():
        sp[1] = ext_got[:, 7, :].T
        sp[2] = ext_got[:, 6, :].T

    for i in range(8):
        t0 = i + 1 if i < 7 else 15
        t15 = i + 8 if i < 7 else 0
        lo, hi = SEG + TAIL * i, SEG + TAIL * (i + 1)
        vv[t0, SEG - TAIL : SEG] = sp[0, lo:hi]
        vv[t15, SEG - TAIL : SEG] = sp[1, lo:hi]

    e_in = pltpu.roll(sp[0, COLS - 5 : COLS + 19], 127, 1)
    w_in = pltpu.roll(sp[1, COLS - 5 : COLS + 19], 1, 1)
    for t in range(WIN):
        sw = rows_s[lat, CHUNK * jj + t]
        if t in (0, WIN - 1):
            u0 = sp[t // (WIN - 1), COLS + WIN : COLS + WIN + 1]
            u44 = sp[t // (WIN - 1), COLS + WIN + 1 : COLS + WIN + 2]
        else:
            u0, u44 = uu[t, 0:1], uu[t, SEG - 1 : SEG]
        r = 5 + 15 - t
        tt[t, SEG - 1 : SEG] += (0.02 * sw - 0.05 * sw * u44) * e_in[r : r + 1]
        tt[t, 0:1] += (0.02 * sw + 0.05 * sw * u0) * w_in[r : r + 1]
    opp = 0.05 * pltpu.roll(sp[2, 0:C8], SEGS // 2, 1)[:SEG]
    tt[0, 0:SEG] -= jnp.where(north_pole, vv[0, 0:SEG] * opp, 0.0)
    tt[WIN - 1, 0:SEG] += jnp.where(south_pole, vv[WIN - 1, 0:SEG] * opp, 0.0)

    col = lax.broadcasted_iota(jnp.int32, (C8, 128), 0)
    m_lane = lax.rem(lax.broadcasted_iota(jnp.int32, (1, KMAX), 1), KMAX // 2)
    o_lane = jnp.where(m_lane == 0, KMAX // 2, KMAX - m_lane)
    w_m = jnp.where(m_lane == 0, 1.0 / (SEG * SEGS), 2.0 / (SEG * SEGS))
    w_o = 2.0 / (SEG * SEGS)

    def lap(old, t):
        g = old[t]
        g8 = pltpu.roll(g[0:8], 127, 1)
        g40 = pltpu.roll(g[40:48], 1, 1)
        e = jnp.where(col == SEG - 1, jnp.broadcast_to(g8[0:1], (C8, 128)), pltpu.roll(g, C8 - 1, 0))
        w = jnp.where(col == 0, jnp.broadcast_to(g40[4:5], (C8, 128)), pltpu.roll(g, 1, 0))
        n = old[max(t - 1, 0)]
        s = old[min(t + 1, WIN - 1)]
        if t == 0:
            n = jnp.where(north_pole, pltpu.roll(g, SEGS // 2, 1), n)
        if t == WIN - 1:
            s = jnp.where(south_pole, pltpu.roll(g, SEGS // 2, 1), s)
        return tend(g, e, w, n, s, uu[t], vv[t], rows_s[lat, CHUNK * jj + t])

    def fold(z, table):
        p = jnp.sum(z * table, axis=0, keepdims=True)
        return p + pltpu.roll(p, KMAX // 2, 1)

    def substep(step, old, new, block):
        ts = range(4 * block, 4 * block + 4)
        raw = [tt[t] if step == 0 else tt[t] + lap(old, t) for t in ts]
        z = product(jnp.concatenate(raw, axis=0), fwd)
        modes = []
        for i, t in enumerate(ts):
            zt = z[C8 * i : C8 * (i + 1)]
            x = CHUNK * jj + t - 4 * lat
            cut = cuts[lat, jnp.minimum(jnp.maximum(x, 0), CAP - 1)]
            km = jnp.where(m_lane <= cut, w_m, 0.0)
            ko = jnp.where(o_lane <= cut, w_o, 0.0)
            modes.append(
                (fold(zt, twiddle[0]) * km) * twiddle[0]
                + (fold(zt, twiddle[1]) * km) * twiddle[1]
                + (fold(zt, twiddle[2]) * ko) * twiddle[2]
                + (fold(zt, twiddle[3]) * ko) * twiddle[3]
            )
        y = product(jnp.concatenate(modes, axis=0), inv)
        for i, t in enumerate(ts):
            x = CHUNK * jj + t - 4 * lat
            inside = jnp.logical_and(x >= 0, x < CAP)
            g = jnp.where(inside, y[C8 * i : C8 * (i + 1)], raw[i])
            new[t] = g if step == 0 else old[t] + g

    for step, (old, new) in enumerate(((gb, ga), (ga, gb), (gb, ga))):
        for block in range(WIN // 4):
            substep(step, old, new, block)
        if step == 0:
            for c in mids:
                c.wait()
            for l in range(LEV):
                for ref, src, a, n in parts:
                    ref[l, 3 - n : 3, pl.ds(own, MW - 128)] = mgot_w[l, a : a + n]
                    ref[l, 3 + SEG : 3 + SEG + n, pl.ds(own, MW - 128)] = mgot_e[l, a : a + n]
            for c in lats:
                c.start()

    for i in range(CHUNK):
        st[SEG * i : SEG * (i + 1)] = ga[2 + i, 0:SEG]
    for i in range(2):
        st[SEG * (CHUNK + i) : SEG * (CHUNK + i + 1)] = jnp.where(lat == 0, ga[i, 0:SEG], ga[WIN - 2 + i, 0:SEG])
    st[SEG * (CHUNK + 2) :] = jnp.zeros((128 * RET - SEG * (CHUNK + 2), 128), F32)
    for p in range(RET):
        ret[:, p, :] = st[128 * p : 128 * (p + 1)].T

    def send_back(d):
        return remote(ret.at[d], back.at[lon], b_s, b_r, at(d))

    spread(send_back)
    back[lon] = ret[lon]

    for c in lats:
        c.wait()
    smid = mid_s[lat]

    @pl.loop(0, LEV)
    def _(l):
        for _ in range(3):
            x = fm[l]
            t = tend(
                x, pltpu.roll(x, 55, 0), pltpu.roll(x, 1, 0),
                pltpu.roll(x, 1, 1), pltpu.roll(x, MW - 1, 1), um[l], vm[l], smid,
            )
            fm[l] = x + t

    @pl.loop(0, LEV)
    def _(l):
        out[l, :, pl.ds(mid0, MW - 128)] = fm[l, 3 : 3 + SEG, pl.ds(own, MW - 128)]

    total(b_r, back, SEGS - 1)
    rl[:, CAP:CW] = jnp.zeros((LEV, CW - CAP, 128), F32)
    lane128 = lax.broadcasted_iota(jnp.int32, (SEGS, 128), 1)
    for i in range(CHUNK + 2):
        p, off = divmod(SEG * i, 128)
        r = back[:, p, :]
        if off:
            r = pltpu.roll(r, 128 - off, 1)
        if off + SEG > 128:
            r = jnp.where(lane128 < 128 - off, r, pltpu.roll(back[:, p + 1, :], 128 - off, 1))
        for l in range(LEV):
            if i < CHUNK:
                rl[l, pl.ds(2 + i, PER, stride=CHUNK), :] = r[PER * l : PER * (l + 1)]
            else:
                rl[l, i - CHUNK : i - CHUNK + 1] = r[PER * l : PER * l + 1]
                rl[l, CAP + 2 + i - CHUNK : CAP + 3 + i - CHUNK] = r[PER * (l + 1) - 1 : PER * (l + 1)]

    for l in range(LEV):
        add = jnp.concatenate([rl[l, 128 * b : 128 * (b + 1)].T[0:C8] for b in range(CW // 128)], axis=1)
        add = pltpu.roll(add, lat * SHIFT, 1)[0:SEG]
        x = lane1 - lat * SHIFT
        inside = jnp.logical_and(x >= 2 * lat, x < CAP + 2 + 2 * lat)
        old = out[l, :, pl.ds(cap0, CW)]
        out[l, :, pl.ds(cap0, CW)] = jnp.where(inside, f[l, :, pl.ds(cap0, CW)] + add, old)

    total(a_s, msg, SEGS - 1)
    total(b_s, ret, SEGS - 1)
    for l in range(LEV):
        d, c = send_ext(l)

        @pl.when(d != lon)
        def _():
            c.wait_send()


def body(f, u, v, cutoffs):
    cap_s, mid_s, rows_s = stretch_table()
    vmem = pl.BlockSpec(memory_space=pltpu.VMEM)
    smem = pl.BlockSpec(memory_space=pltpu.SMEM)
    V = lambda *shape: pltpu.VMEM(shape, F32)
    dma = pltpu.SemaphoreType.DMA
    return pl.pallas_call(
        kernel,
        out_shape=jax.ShapeDtypeStruct(f.shape, F32),
        in_specs=[pl.BlockSpec(memory_space=pl.ANY)] * 3 + [smem] * 2 + [vmem] * 5,
        out_specs=vmem,
        scratch_shapes=[
            V(LEV, SEG, ROWS), V(LEV, SEG, ROWS), V(LEV, SEG, ROWS),
            V(LEV, 8, MW - 128), V(LEV, 8, MW - 128), V(LEV, 8, MW - 128), V(LEV, 8, MW - 128),
            V(LEV, 56, MW), V(LEV, 56, MW), V(LEV, 56, MW),
            V(136, CW), V(128, CW), V(CW, 128), V(CW, 128),
            V(SEGS, WIN, 128), V(SEGS, WIN, 128), V(LEV, 8, 128), V(SEGS, 8, 128), V(3, 128, 128),
            V(WIN, C8, 128), V(WIN, C8, 128), V(WIN, C8, 128), V(WIN, C8, 128), V(WIN, C8, 128),
            V(128 * RET, 128), V(SEGS, RET, 128), V(SEGS, RET, 128), V(LEV, CW, 128),
            dma((3,)), dma((3,)), dma((2,)), dma((2,)), dma((3,)), dma((3,)),
            dma, dma, dma((LEV,)), dma, dma, dma,
        ],
        compiler_params=pltpu.CompilerParams(
            collective_id=0, has_side_effects=True, vmem_limit_bytes=40 * 1024 * 1024
        ),
    )(f, u, v, cutoffs, rows_s, cap_s, mid_s, *tables())


def solution(mesh):
    placed = (P(None, "lon", "lat"), P(None, "lon", "lat"), P(None, "lon", "lat"), P())
    return jax.shard_map(
        body, mesh=mesh, in_specs=placed, out_specs=P(None, "lon", "lat"), check_vma=False
    )
```

```python
import functools
import math

import jax
import jax.numpy as jnp
import ml_dtypes
import numpy as np
from jax import lax
from jax.experimental import pallas as pl
from jax.experimental.pallas import tpu as pltpu
from jax.sharding import PartitionSpec as P

MESH = pl.DeviceIdType.MESH
LEV, SEG, ROWS, SEGS = 4, 45, 1152, 128
CAP = ROWS // 3
CHUNK, WIN = 12, 16
PER = CAP // CHUNK
CW = 512
SHIFT = CW - CAP - 4
MW = 1024
KMAX = 128
C8 = 48
RET = 5
COLS = 101
TAIL = 7
F32, BF16 = jnp.float32, jnp.bfloat16


def split(x):
    hi = x.astype(ml_dtypes.bfloat16)
    return hi, (x - hi.astype(np.float32)).astype(ml_dtypes.bfloat16)


def two_parts(basis):
    hi, lo = split(np.ascontiguousarray(basis))
    return np.concatenate(
        [np.concatenate([hi, lo], axis=1), np.concatenate([hi, np.zeros_like(lo)], axis=1)], axis=0
    )


def tables():
    total = SEG * SEGS
    half = KMAX // 2
    m, s, c = np.arange(half), np.arange(SEGS), np.arange(SEG)
    a = 2 * np.pi * ((s[:, None] * m[None, :]) % SEGS) / SEGS
    sin = np.sin(a)
    sin[:, 0] = np.where(s % 2 == 0, 1.0, -1.0)
    basis = np.concatenate([np.cos(a), sin], axis=1).astype(np.float32)
    other = np.where(m == 0, half, KMAX - m)
    angle = lambda k: 2 * np.pi * (c[:, None] * k[None, :]) / total
    cm, sm, co, so = np.cos(angle(m)), np.sin(angle(m)), np.cos(angle(other)), np.sin(angle(other))
    ta, tb = np.concatenate([cm, -sm], axis=1), np.concatenate([sm, cm], axis=1)
    pa, pb = np.concatenate([co, so], axis=1), np.concatenate([so, -co], axis=1)
    ta[:, half], tb[:, half], pa[:, 0], pb[:, 0] = 0.0, 0.0, 0.0, 0.0
    pa[:, half], pb[:, half] = co[:, 0], so[:, 0]
    twiddle = np.pad(np.stack([ta, tb, pa, pb]), ((0, 0), (0, C8 - SEG), (0, 0))).astype(np.float32)
    return two_parts(basis), two_parts(basis.T), twiddle


def stretch_table():
    colat = np.float32(math.pi) * (np.arange(2 * ROWS).astype(np.float32) + np.float32(0.5))
    colat = (colat / np.float32(2 * ROWS)).astype(np.float32)
    s = np.float32(1.0) / np.maximum(np.sin(colat), np.float32(0.125))
    s = np.pad(s.astype(np.float32), (0, MW))
    cap = np.stack([s[:CW], s[2 * ROWS - CW : 2 * ROWS]])[:, None, :]
    mid = np.stack([s[256 : 256 + MW], s[ROWS - 128 : ROWS - 128 + MW]])[:, None, :]
    rows = np.stack([s[: CAP + 4], s[2 * ROWS - CAP - 4 : 2 * ROWS]])
    return cap, mid, rows


def tend(mid, east, west, north, south, u, v, s):
    return (
        -0.05 * s * u * (east - west)
        - 0.05 * v * (north - south)
        + 0.02 * s * (east - 2.0 * mid + west)
    )


def product(x, parts_ref):
    hi = x.astype(BF16)
    lo = (x - hi.astype(F32)).astype(BF16)
    r = jnp.dot(jnp.concatenate([hi, lo], axis=1), parts_ref[...], preferred_element_type=F32)
    return r[:, 0:128] + r[:, 128:]


def kernel(
    f_hbm, u_hbm, v_hbm, cuts, rows_s, cap_s, mid_s, fwd, inv, twiddle,
    out_hbm,
    out, f, u, v, mid_w, mid_e, mgot_w, mgot_e,
    fm, um, vm, mm, mx, ln, lx, msg, recv, ext, ext_got, sp,
    tt, uu, vv, ga, gb, st, ret, back, rl,
    d_s, cs, os, ms, mr, ls, lr, a_s, a_r, x_s, x_r, b_s, b_r,
):
    lat = lax.axis_index("lat")
    lon = lax.axis_index("lon")
    south = lat == 1
    jj = lax.rem(lon, PER)
    north_pole = jnp.logical_and(lat == 0, jj == 0)
    south_pole = jnp.logical_and(lat == 1, jj == PER - 1)
    at = lambda d: (lat, d)
    east_dev = at(lax.rem(lon + 1, SEGS))
    west_dev = at(lax.rem(lon + SEGS - 1, SEGS))
    partner = (1 - lat, lon)

    cap0 = pl.multiple_of(lat * (ROWS - CW), 128)
    mid0 = pl.multiple_of((1 - lat) * 256, 128)
    rest0 = pl.multiple_of((1 - lat) * CW, 128)
    pairs = ((f_hbm, f), (u_hbm, u), (v_hbm, v))

    def load(i, l, first, lanes, sems):
        src, dst = pairs[i]
        return pltpu.make_async_copy(
            src.at[:, l, pl.ds(first, lanes)], dst.at[l, :, pl.ds(first, lanes)], sems.at[i, l]
        )

    others = [load(i, l, rest0, ROWS - CW, os) for l in range(LEV) for i in range(3)]
    for l in range(LEV):
        for i in range(3):
            load(i, l, cap0, CW, cs).start()

    barrier = pltpu.get_barrier_semaphore()

    def greet(k):
        pl.semaphore_signal(barrier, inc=1, device_id=at(lax.rem(lon + k, SEGS)), device_id_type=MESH)

    @pl.loop(0, (SEGS - 1) // 8)
    def _(k):
        for i in range(8):
            greet(8 * k + i + 1)

    for k in range((SEGS - 1) // 8 * 8 + 1, SEGS):
        greet(k)
    pl.semaphore_signal(barrier, inc=1, device_id=partner, device_id_type=MESH)

    for c in others:
        c.start()

    lanes = lax.broadcasted_iota(jnp.int32, (C8, CW), 1)
    scap = cap_s[lat]
    row = lax.broadcasted_iota(jnp.int32, (WIN, 128), 0)
    lane1 = lanes[:SEG]
    pole = jnp.where(lat == 0, 0, CW - 1)

    @pl.loop(0, LEV)
    def _(l):
        for i in range(3):
            load(i, l, cap0, CW, cs).wait()
        fc = f[l, :, pl.ds(cap0, CW)]
        uc = u[l, :, pl.ds(cap0, CW)]
        vc = v[l, :, pl.ds(cap0, CW)]
        zero = jnp.zeros((1, CW), F32)
        e = jnp.concatenate([fc[1:], zero], axis=0)
        w = jnp.concatenate([zero, fc[:-1]], axis=0)
        n = jnp.where(jnp.logical_and(lane1 == pole, lat == 0), 0.0, pltpu.roll(fc, 1, 1))
        s = jnp.where(jnp.logical_and(lane1 == pole, lat == 1), 0.0, pltpu.roll(fc, CW - 1, 1))
        turn = lax.rem(CW - lat * SHIFT, CW)
        mm[0:SEG] = pltpu.roll(tend(fc, e, w, n, s, uc, vc, scap), turn, 1)
        mm[SEG : 2 * SEG] = pltpu.roll(uc, turn, 1)
        mm[2 * SEG : 3 * SEG] = pltpu.roll(vc, turn, 1)
        vt = mm[128 : 128 + TAIL]
        x12 = lax.rem(lanes[:WIN], 12)
        edge = pltpu.roll(fc, lax.rem(CW - lat * (SHIFT + 2) + 1, CW), 1)
        mx[0:SEG] = jnp.where(lane1 == jnp.where(lat == 0, 1, CAP + 2), edge, mm[0:SEG])
        for i in range(8):
            t0 = i + 1 if i < 7 else 15
            t15 = i + 8 if i < 7 else 0
            a0 = pltpu.roll(vt, CW - t0, 1)
            a15 = pltpu.roll(vt, 15 - t15, 1)
            mx[SEG + TAIL * i : SEG + TAIL * (i + 1)] = jnp.where(x12[:TAIL] == 3, a15, a0)
        ft = pltpu.roll(fc, turn, 1)
        f0 = jnp.broadcast_to(ft[0:1], (WIN, CW))
        f44 = jnp.broadcast_to(ft[SEG - 1 : SEG], (WIN, CW))
        f0 = pltpu.roll(f0, CW - 15, 1, stride=1, stride_axis=0)
        f44 = pltpu.roll(f44, 0, 1, stride=1, stride_axis=0)
        mx[COLS : COLS + WIN] = jnp.where(x12 == 3, f44, f0)
        mx[COLS + WIN : COLS + WIN + 1] = mm[SEG : SEG + 1]
        mx[COLS + WIN + 1 : COLS + WIN + 2] = mm[2 * SEG - 1 : 2 * SEG]
        for b in range(CW // 128):
            ln[128 * b : 128 * (b + 1)] = mm[0:128, 128 * b : 128 * (b + 1)].T
            lx[128 * b : 128 * (b + 1)] = mx[0:128, 128 * b : 128 * (b + 1)].T

        @pl.loop(0, PER // 8)
        def _(mo):
            for mi in range(4):
                m = 4 * mo + mi
                a = ln[pl.ds(pl.multiple_of(24 * m, 8), 32)]
                b = lx[pl.ds(pl.multiple_of(24 * m, 8), 32)]
                first = jnp.logical_and(m == 0, lat == 0)
                last = jnp.logical_and(m == PER // 2 - 1, lat == 1)
                use0 = jnp.logical_or(jnp.logical_and(row == 0, jnp.logical_not(first)), row == WIN - 1)
                use1 = jnp.logical_or(row == 0, jnp.logical_and(row == WIN - 1, jnp.logical_not(last)))
                msg[l * PER + 2 * m] = jnp.where(use0, b[0:16], a[0:16])
                msg[l * PER + 2 * m + 1] = jnp.where(use1, b[12:28], a[12:28])

        ext[l] = jnp.where(lat == 0, lx[0:8], lx[CAP - 4 : CAP + 4])

    pl.semaphore_wait(barrier, SEGS)

    def remote(src, dst, send, recv_sem, dev):
        return pltpu.make_async_remote_copy(
            src_ref=src, dst_ref=dst, send_sem=send, recv_sem=recv_sem,
            device_id=dev, device_id_type=MESH,
        )

    def send_line(d):
        return remote(msg.at[d], recv.at[lon], a_s, a_r, at(d))

    def spread(send):
        @pl.loop(0, (SEGS // 2 - 1) // 7)
        def _(k):
            for i in range(1, 8):
                send(lax.rem(lon + 7 * k + i, SEGS)).start()
                send(lax.rem(lon + SEGS - 7 * k - i, SEGS)).start()

        send(lax.rem(lon + SEGS // 2, SEGS)).start()

    spread(send_line)
    recv[lon] = msg[lon]

    def send_ext(l):
        d = l * PER + lat * (PER - 1)
        return d, remote(ext.at[l], ext_got.at[lon], x_s.at[l], x_r, at(d))

    for l in range(LEV):
        d, c = send_ext(l)

        @pl.when(d != lon)
        def _():
            c.start()

        @pl.when(d == lon)
        def _():
            ext_got[lon] = ext[l]

    for c in others:
        c.wait()
    own = pl.multiple_of(lat * 128, 128)
    mid_w[...] = jnp.zeros_like(mid_w)
    mid_e[...] = jnp.zeros_like(mid_e)
    parts = ((fm, f, 0, 3), (um, u, 3, 2), (vm, v, 5, 2))
    for l in range(LEV):
        for ref, src, a, n in parts:
            mid_w[l, a : a + n] = src[l, 0:n, pl.ds(mid0, MW - 128)]
            mid_e[l, a : a + n] = src[l, SEG - n : SEG, pl.ds(mid0, MW - 128)]

    @pl.loop(0, LEV)
    def _(l):
        for ref, src, a, n in parts:
            ref[l, 3 : 3 + SEG, pl.ds(own, MW - 128)] = src[l, :, pl.ds(mid0, MW - 128)]

    mids = [
        remote(mid_w, mgot_e, ms.at[0], mr.at[0], west_dev),
        remote(mid_e, mgot_w, ms.at[1], mr.at[1], east_dev),
    ]
    src0 = pl.multiple_of((1 - lat) * (MW - 256) + lat * 128, 128)
    dst0 = pl.multiple_of(lat * (MW - 128), 128)
    lats = [
        remote(ref.at[:, :, pl.ds(src0, 128)], ref.at[:, :, pl.ds(dst0, 128)], ls.at[i], lr.at[i], partner)
        for i, ref in enumerate((fm, um, vm))
    ]

    def total(sem, ref, n):
        pltpu.make_async_copy(ref.at[pl.ds(0, n)], ref.at[pl.ds(0, n)], sem).wait()

    total(a_s, msg, SEGS - 1)
    for c in mids:
        c.start()
    total(a_r, recv, SEGS - 1)
    tt[:, SEG:C8] = jnp.zeros((WIN, C8 - SEG, 128), F32)
    uu[:, SEG:C8] = jnp.zeros((WIN, C8 - SEG, 128), F32)
    vv[:, SEG:C8] = jnp.zeros((WIN, C8 - SEG, 128), F32)
    for t in range(WIN):
        w = recv[:, t, :].T
        tt[t, 0:SEG] = w[0:SEG]
        uu[t, 0:SEG] = w[SEG : 2 * SEG]
        vv[t, 0 : SEG - TAIL] = w[2 * SEG : 128]
        if t == 0:
            sp[0] = w
        if t == WIN - 1:
            sp[1] = w

    @pl.when(jnp.logical_or(north_pole, south_pole))
    def _():
        total(x_r, ext_got, SEGS - 1)

    sp[2] = jnp.zeros((128, 128), F32)

    @pl.when(north_pole)
    def _():
        sp[0] = ext_got[:, 0, :].T
        sp[2] = ext_got[:, 1, :].T

    @pl.when(south_pole)
    def _():
        sp[1] = ext_got[:, 7, :].T
        sp[2] = ext_got[:, 6, :].T

    for i in range(8):
        t0 = i + 1 if i < 7 else 15
        t15 = i + 8 if i < 7 else 0
        lo, hi = SEG + TAIL * i, SEG + TAIL * (i + 1)
        vv[t0, SEG - TAIL : SEG] = sp[0, lo:hi]
        vv[t15, SEG - TAIL : SEG] = sp[1, lo:hi]

    e_in = pltpu.roll(sp[0, COLS - 5 : COLS + 19], 127, 1)
    w_in = pltpu.roll(sp[1, COLS - 5 : COLS + 19], 1, 1)
    for t in range(WIN):
        sw = rows_s[lat, CHUNK * jj + t]
        if t in (0, WIN - 1):
            u0 = sp[t // (WIN - 1), COLS + WIN : COLS + WIN + 1]
            u44 = sp[t // (WIN - 1), COLS + WIN + 1 : COLS + WIN + 2]
        else:
            u0, u44 = uu[t, 0:1], uu[t, SEG - 1 : SEG]
        r = 5 + 15 - t
        tt[t, SEG - 1 : SEG] += (0.02 * sw - 0.05 * sw * u44) * e_in[r : r + 1]
        tt[t, 0:1] += (0.02 * sw + 0.05 * sw * u0) * w_in[r : r + 1]
    opp = 0.05 * pltpu.roll(sp[2, 0:C8], SEGS // 2, 1)[:SEG]
    tt[0, 0:SEG] -= jnp.where(north_pole, vv[0, 0:SEG] * opp, 0.0)
    tt[WIN - 1, 0:SEG] += jnp.where(south_pole, vv[WIN - 1, 0:SEG] * opp, 0.0)

    col = lax.broadcasted_iota(jnp.int32, (C8, 128), 0)
    m_lane = lax.rem(lax.broadcasted_iota(jnp.int32, (1, KMAX), 1), KMAX // 2)
    o_lane = jnp.where(m_lane == 0, KMAX // 2, KMAX - m_lane)
    w_m = jnp.where(m_lane == 0, 1.0 / (SEG * SEGS), 2.0 / (SEG * SEGS))
    w_o = 2.0 / (SEG * SEGS)

    def lap(old, t):
        g = old[t]
        g8 = pltpu.roll(g[0:8], 127, 1)
        g40 = pltpu.roll(g[40:48], 1, 1)
        e = jnp.where(col == SEG - 1, jnp.broadcast_to(g8[0:1], (C8, 128)), pltpu.roll(g, C8 - 1, 0))
        w = jnp.where(col == 0, jnp.broadcast_to(g40[4:5], (C8, 128)), pltpu.roll(g, 1, 0))
        n = old[max(t - 1, 0)]
        s = old[min(t + 1, WIN - 1)]
        if t == 0:
            n = jnp.where(north_pole, pltpu.roll(g, SEGS // 2, 1), n)
        if t == WIN - 1:
            s = jnp.where(south_pole, pltpu.roll(g, SEGS // 2, 1), s)
        return tend(g, e, w, n, s, uu[t], vv[t], rows_s[lat, CHUNK * jj + t])

    def fold(z, table):
        p = jnp.sum(z * table, axis=0, keepdims=True)
        return p + pltpu.roll(p, KMAX // 2, 1)

    def substep(step, old, new, block):
        ts = range(4 * block, 4 * block + 4)
        raw = [tt[t] if step == 0 else tt[t] + lap(old, t) for t in ts]
        z = product(jnp.concatenate(raw, axis=0), fwd)
        modes = []
        for i, t in enumerate(ts):
            zt = z[C8 * i : C8 * (i + 1)]
            x = CHUNK * jj + t - 4 * lat
            cut = cuts[lat, jnp.minimum(jnp.maximum(x, 0), CAP - 1)]
            km = jnp.where(m_lane <= cut, w_m, 0.0)
            ko = jnp.where(o_lane <= cut, w_o, 0.0)
            modes.append(
                (fold(zt, twiddle[0]) * km) * twiddle[0]
                + (fold(zt, twiddle[1]) * km) * twiddle[1]
                + (fold(zt, twiddle[2]) * ko) * twiddle[2]
                + (fold(zt, twiddle[3]) * ko) * twiddle[3]
            )
        y = product(jnp.concatenate(modes, axis=0), inv)
        for i, t in enumerate(ts):
            x = CHUNK * jj + t - 4 * lat
            inside = jnp.logical_and(x >= 0, x < CAP)
            g = jnp.where(inside, y[C8 * i : C8 * (i + 1)], raw[i])
            new[t] = g if step == 0 else old[t] + g

    for step, (old, new) in enumerate(((gb, ga), (ga, gb), (gb, ga))):
        for block in range(WIN // 4):
            substep(step, old, new, block)

    for i in range(CHUNK):
        st[SEG * i : SEG * (i + 1)] = ga[2 + i, 0:SEG]
    for i in range(2):
        st[SEG * (CHUNK + i) : SEG * (CHUNK + i + 1)] = jnp.where(lat == 0, ga[i, 0:SEG], ga[WIN - 2 + i, 0:SEG])
    st[SEG * (CHUNK + 2) :] = jnp.zeros((128 * RET - SEG * (CHUNK + 2), 128), F32)
    for p in range(RET):
        ret[:, p, :] = st[128 * p : 128 * (p + 1)].T

    def send_back(d):
        return remote(ret.at[d], back.at[lon], b_s, b_r, at(d))

    spread(send_back)
    back[lon] = ret[lon]
    for c in mids:
        c.wait()
    for l in range(LEV):
        for ref, src, a, n in parts:
            ref[l, 3 - n : 3, pl.ds(own, MW - 128)] = mgot_w[l, a : a + n]
            ref[l, 3 + SEG : 3 + SEG + n, pl.ds(own, MW - 128)] = mgot_e[l, a : a + n]
    for c in lats:
        c.start()

    for c in lats:
        c.wait()
    smid = mid_s[lat]

    @pl.loop(0, LEV)
    def _(l):
        for _ in range(3):
            x = fm[l]
            t = tend(
                x, pltpu.roll(x, 55, 0), pltpu.roll(x, 1, 0),
                pltpu.roll(x, 1, 1), pltpu.roll(x, MW - 1, 1), um[l], vm[l], smid,
            )
            fm[l] = x + t

    @pl.loop(0, LEV)
    def _(l):
        out[l, :, pl.ds(mid0, MW - 128)] = fm[l, 3 : 3 + SEG, pl.ds(own, MW - 128)]

    total(b_r, back, SEGS - 1)
    rl[:, CAP:CW] = jnp.zeros((LEV, CW - CAP, 128), F32)
    lane128 = lax.broadcasted_iota(jnp.int32, (SEGS, 128), 1)
    for i in range(CHUNK + 2):
        p, off = divmod(SEG * i, 128)
        r = back[:, p, :]
        if off:
            r = pltpu.roll(r, 128 - off, 1)
        if off + SEG > 128:
            r = jnp.where(lane128 < 128 - off, r, pltpu.roll(back[:, p + 1, :], 128 - off, 1))
        for l in range(LEV):
            if i < CHUNK:
                rl[l, pl.ds(2 + i, PER, stride=CHUNK), :] = r[PER * l : PER * (l + 1)]
            else:
                rl[l, i - CHUNK : i - CHUNK + 1] = r[PER * l : PER * l + 1]
                rl[l, CAP + 2 + i - CHUNK : CAP + 3 + i - CHUNK] = r[PER * (l + 1) - 1 : PER * (l + 1)]

    stores = [pltpu.make_async_copy(out.at[l], out_hbm.at[:, l, :], d_s.at[l]) for l in range(LEV)]
    for l in range(LEV):
        add = jnp.concatenate([rl[l, 128 * b : 128 * (b + 1)].T[0:C8] for b in range(CW // 128)], axis=1)
        add = pltpu.roll(add, lat * SHIFT, 1)[0:SEG]
        x = lane1 - lat * SHIFT
        inside = jnp.logical_and(x >= 2 * lat, x < CAP + 2 + 2 * lat)
        old = out[l, :, pl.ds(cap0, CW)]
        out[l, :, pl.ds(cap0, CW)] = jnp.where(inside, f[l, :, pl.ds(cap0, CW)] + add, old)
        stores[l].start()

    total(b_s, ret, SEGS - 1)
    for l in range(LEV):
        d, c = send_ext(l)

        @pl.when(d != lon)
        def _():
            c.wait_send()

    for c in stores:
        c.wait()


def body(f, u, v, cutoffs):
    cap_s, mid_s, rows_s = stretch_table()
    vmem = pl.BlockSpec(memory_space=pltpu.VMEM)
    smem = pl.BlockSpec(memory_space=pltpu.SMEM)
    V = lambda *shape: pltpu.VMEM(shape, F32)
    dma = pltpu.SemaphoreType.DMA
    f, u, v = (jnp.transpose(a, (1, 0, 2)) for a in (f, u, v))
    done = pl.pallas_call(
        kernel,
        out_shape=jax.ShapeDtypeStruct(f.shape, F32),
        in_specs=[pl.BlockSpec(memory_space=pl.ANY)] * 3 + [smem] * 2 + [vmem] * 5,
        out_specs=pl.BlockSpec(memory_space=pl.ANY),
        scratch_shapes=[
            V(LEV, SEG, ROWS), V(LEV, SEG, ROWS), V(LEV, SEG, ROWS), V(LEV, SEG, ROWS),
            V(LEV, 8, MW - 128), V(LEV, 8, MW - 128), V(LEV, 8, MW - 128), V(LEV, 8, MW - 128),
            V(LEV, 56, MW), V(LEV, 56, MW), V(LEV, 56, MW),
            V(136, CW), V(128, CW), V(CW, 128), V(CW, 128),
            V(SEGS, WIN, 128), V(SEGS, WIN, 128), V(LEV, 8, 128), V(SEGS, 8, 128), V(3, 128, 128),
            V(WIN, C8, 128), V(WIN, C8, 128), V(WIN, C8, 128), V(WIN, C8, 128), V(WIN, C8, 128),
            V(128 * RET, 128), V(SEGS, RET, 128), V(SEGS, RET, 128), V(LEV, CW, 128),
            dma((LEV,)), dma((3, LEV)), dma((3, LEV)), dma((2,)), dma((2,)), dma((3,)), dma((3,)),
            dma, dma, dma((LEV,)), dma, dma, dma,
        ],
        compiler_params=pltpu.CompilerParams(
            collective_id=0, has_side_effects=True, vmem_limit_bytes=60 * 1024 * 1024
        ),
    )(f, u, v, cutoffs, rows_s, cap_s, mid_s, *tables())
    return jnp.transpose(done, (1, 0, 2))


def solution(mesh):
    placed = (P(None, "lon", "lat"), P(None, "lon", "lat"), P(None, "lon", "lat"), P())
    return jax.shard_map(
        body, mesh=mesh, in_specs=placed, out_specs=P(None, "lon", "lat"), check_vma=False
    )
```

```python
import functools
import math

import jax
import jax.numpy as jnp
import ml_dtypes
import numpy as np
from jax import lax
from jax.experimental import pallas as pl
from jax.experimental.pallas import tpu as pltpu
from jax.sharding import PartitionSpec as P

MESH = pl.DeviceIdType.MESH
LEV, SEG, ROWS, SEGS = 4, 45, 1152, 128
CAP = ROWS // 3
CHUNK, WIN = 12, 16
PER = CAP // CHUNK
CW = 512
SHIFT = CW - CAP - 4
MW = 1024
KMAX = 128
C8 = 48
BLOCK = 16
RET = 5
SMALL = 7
COLS = 101
TAIL = 7
F32, BF16 = jnp.float32, jnp.bfloat16


def split(x):
    hi = x.astype(ml_dtypes.bfloat16)
    return hi, (x - hi.astype(np.float32)).astype(ml_dtypes.bfloat16)


def two_parts(basis):
    hi, lo = split(np.ascontiguousarray(basis))
    return np.concatenate(
        [np.concatenate([hi, lo], axis=1), np.concatenate([hi, np.zeros_like(lo)], axis=1)], axis=0
    )


def tables():
    total = SEG * SEGS
    half = KMAX // 2
    m, s, c = np.arange(half), np.arange(SEGS), np.arange(SEG)
    a = 2 * np.pi * ((s[:, None] * m[None, :]) % SEGS) / SEGS
    sin = np.sin(a)
    sin[:, 0] = np.where(s % 2 == 0, 1.0, -1.0)
    basis = np.concatenate([np.cos(a), sin], axis=1).astype(np.float32)
    other = np.where(m == 0, half, KMAX - m)
    angle = lambda k: 2 * np.pi * (c[:, None] * k[None, :]) / total
    cm, sm, co, so = np.cos(angle(m)), np.sin(angle(m)), np.cos(angle(other)), np.sin(angle(other))
    ta, tb = np.concatenate([cm, -sm], axis=1), np.concatenate([sm, cm], axis=1)
    pa, pb = np.concatenate([co, so], axis=1), np.concatenate([so, -co], axis=1)
    ta[:, half], tb[:, half], pa[:, 0], pb[:, 0] = 0.0, 0.0, 0.0, 0.0
    pa[:, half], pb[:, half] = co[:, 0], so[:, 0]
    twiddle = np.pad(np.stack([ta, tb, pa, pb]), ((0, 0), (0, C8 - SEG), (0, 0))).astype(np.float32)
    return two_parts(basis), two_parts(basis.T), twiddle


def stretch_table():
    colat = np.float32(math.pi) * (np.arange(2 * ROWS).astype(np.float32) + np.float32(0.5))
    colat = (colat / np.float32(2 * ROWS)).astype(np.float32)
    s = np.float32(1.0) / np.maximum(np.sin(colat), np.float32(0.125))
    s = np.pad(s.astype(np.float32), (0, MW))
    cap = np.stack([s[:CW], s[2 * ROWS - CW : 2 * ROWS]])[:, None, :]
    mid = np.stack([s[256 : 256 + MW], s[ROWS - 128 : ROWS - 128 + MW]])[:, None, :]
    rows = np.stack([s[: CAP + 4], s[2 * ROWS - CAP - 4 : 2 * ROWS]])
    return cap, mid, rows


def tend(mid, east, west, north, south, u, v, s):
    return (
        -0.05 * s * u * (east - west)
        - 0.05 * v * (north - south)
        + 0.02 * s * (east - 2.0 * mid + west)
    )


def product(x, parts_ref):
    hi = x.astype(BF16)
    lo = (x - hi.astype(F32)).astype(BF16)
    r = jnp.dot(jnp.concatenate([hi, lo], axis=1), parts_ref[...], preferred_element_type=F32)
    return r[:, 0:128] + r[:, 128:]


def kernel(
    f_hbm, u_hbm, v_hbm, *rest,
):
    small, (out_hbm, *scratch) = rest[:SMALL], rest[SMALL:]
    run(f_hbm, u_hbm, v_hbm, small, out_hbm, *scratch)


def run(
    f_hbm, u_hbm, v_hbm, small, out_hbm,
    cuts, rows_s, cap_s, mid_s, fwd, inv, twiddle, small_s,
    out, f, u, v, mid_w, mid_e, mgot_w, mgot_e,
    fm, um, vm, mm, mx, ln, lx, msg, recv, ext, ext_got, sp,
    tt, uu, vv, ga, gb, st, ret, back, rl,
    d_s, cs, os, ms, mr, ls, lr, a_s, a_r, x_s, x_r, b_s, b_r,
):
    lat = lax.axis_index("lat")
    lon = lax.axis_index("lon")
    south = lat == 1
    jj = lax.rem(lon, PER)
    north_pole = jnp.logical_and(lat == 0, jj == 0)
    south_pole = jnp.logical_and(lat == 1, jj == PER - 1)
    at = lambda d: (lat, d)
    east_dev = at(lax.rem(lon + 1, SEGS))
    west_dev = at(lax.rem(lon + SEGS - 1, SEGS))
    partner = (1 - lat, lon)

    cap0 = pl.multiple_of(lat * (ROWS - CW), 128)
    mid0 = pl.multiple_of((1 - lat) * 256, 128)
    rest0 = pl.multiple_of((1 - lat) * CW, 128)
    pairs = ((f_hbm, f), (u_hbm, u), (v_hbm, v))

    def load(i, l, first, lanes, sems):
        src, dst = pairs[i]
        return pltpu.make_async_copy(
            src.at[:, l, pl.ds(first, lanes)], dst.at[l, :, pl.ds(first, lanes)], sems.at[i, l]
        )

    others = [load(i, l, rest0, ROWS - CW, os) for l in range(LEV) for i in range(3)]
    barrier = pltpu.get_barrier_semaphore()

    def greet(k):
        pl.semaphore_signal(barrier, inc=1, device_id=at(lax.rem(lon + k, SEGS)), device_id_type=MESH)

    @pl.loop(0, (SEGS - 1) // 8)
    def _(k):
        for i in range(8):
            greet(8 * k + i + 1)

    for k in range((SEGS - 1) // 8 * 8 + 1, SEGS):
        greet(k)
    pl.semaphore_signal(barrier, inc=1, device_id=partner, device_id_type=MESH)

    held = (cuts, rows_s, cap_s, mid_s, fwd, inv, twiddle)
    smalls = [pltpu.make_async_copy(src, dst, small_s.at[i]) for i, (src, dst) in enumerate(zip(small, held))]
    for l in range(LEV):
        for i in range(3):
            load(i, l, cap0, CW, cs).start()
        if l == 0:
            smalls[2].start()
    for i, c in enumerate(smalls):
        if i != 2:
            c.start()
    for c in others:
        c.start()
    smalls[2].wait()

    lanes = lax.broadcasted_iota(jnp.int32, (C8, CW), 1)
    scap = cap_s[lat]
    row = lax.broadcasted_iota(jnp.int32, (WIN, 128), 0)
    lane1 = lanes[:SEG]
    pole = jnp.where(lat == 0, 0, CW - 1)

    @pl.loop(0, LEV)
    def _(l):
        for i in range(3):
            load(i, l, cap0, CW, cs).wait()
        fc = f[l, :, pl.ds(cap0, CW)]
        uc = u[l, :, pl.ds(cap0, CW)]
        vc = v[l, :, pl.ds(cap0, CW)]
        zero = jnp.zeros((1, CW), F32)
        e = jnp.concatenate([fc[1:], zero], axis=0)
        w = jnp.concatenate([zero, fc[:-1]], axis=0)
        n = jnp.where(jnp.logical_and(lane1 == pole, lat == 0), 0.0, pltpu.roll(fc, 1, 1))
        s = jnp.where(jnp.logical_and(lane1 == pole, lat == 1), 0.0, pltpu.roll(fc, CW - 1, 1))
        turn = lax.rem(CW - lat * SHIFT, CW)
        mm[0:SEG] = pltpu.roll(tend(fc, e, w, n, s, uc, vc, scap), turn, 1)
        mm[SEG : 2 * SEG] = pltpu.roll(uc, turn, 1)
        mm[2 * SEG : 3 * SEG] = pltpu.roll(vc, turn, 1)
        vt = mm[128 : 128 + TAIL]
        x12 = lax.rem(lanes[:WIN], 12)
        edge = pltpu.roll(fc, lax.rem(CW - lat * (SHIFT + 2) + 1, CW), 1)
        mx[0:SEG] = jnp.where(lane1 == jnp.where(lat == 0, 1, CAP + 2), edge, mm[0:SEG])
        for i in range(8):
            t0 = i + 1 if i < 7 else 15
            t15 = i + 8 if i < 7 else 0
            a0 = pltpu.roll(vt, CW - t0, 1)
            a15 = pltpu.roll(vt, 15 - t15, 1)
            mx[SEG + TAIL * i : SEG + TAIL * (i + 1)] = jnp.where(x12[:TAIL] == 3, a15, a0)
        ft = pltpu.roll(fc, turn, 1)
        f0 = jnp.broadcast_to(ft[0:1], (WIN, CW))
        f44 = jnp.broadcast_to(ft[SEG - 1 : SEG], (WIN, CW))
        f0 = pltpu.roll(f0, CW - 15, 1, stride=1, stride_axis=0)
        f44 = pltpu.roll(f44, 0, 1, stride=1, stride_axis=0)
        mx[COLS : COLS + WIN] = jnp.where(x12 == 3, f44, f0)
        mx[COLS + WIN : COLS + WIN + 1] = mm[SEG : SEG + 1]
        mx[COLS + WIN + 1 : COLS + WIN + 2] = mm[2 * SEG - 1 : 2 * SEG]
        for b in range(CW // 128):
            ln[128 * b : 128 * (b + 1)] = mm[0:128, 128 * b : 128 * (b + 1)].T
            lx[128 * b : 128 * (b + 1)] = mx[0:128, 128 * b : 128 * (b + 1)].T

        @pl.loop(0, PER // 8)
        def _(mo):
            for mi in range(4):
                m = 4 * mo + mi
                a = ln[pl.ds(pl.multiple_of(24 * m, 8), 32)]
                b = lx[pl.ds(pl.multiple_of(24 * m, 8), 32)]
                first = jnp.logical_and(m == 0, lat == 0)
                last = jnp.logical_and(m == PER // 2 - 1, lat == 1)
                use0 = jnp.logical_or(jnp.logical_and(row == 0, jnp.logical_not(first)), row == WIN - 1)
                use1 = jnp.logical_or(row == 0, jnp.logical_and(row == WIN - 1, jnp.logical_not(last)))
                msg[l * PER + 2 * m] = jnp.where(use0, b[0:16], a[0:16])
                msg[l * PER + 2 * m + 1] = jnp.where(use1, b[12:28], a[12:28])

        ext[l] = jnp.where(lat == 0, lx[0:2], lx[CAP + 2 : CAP + 4])

    pl.semaphore_wait(barrier, SEGS)

    def remote(src, dst, send, recv_sem, dev):
        return pltpu.make_async_remote_copy(
            src_ref=src, dst_ref=dst, send_sem=send, recv_sem=recv_sem,
            device_id=dev, device_id_type=MESH,
        )

    def send_line(d):
        return remote(msg.at[d], recv.at[lon], a_s, a_r, at(d))

    def spread(send):
        @pl.loop(0, (SEGS // 2 - 1) // 7)
        def _(k):
            for i in range(1, 8):
                send(lax.rem(lon + 7 * k + i, SEGS)).start()
                send(lax.rem(lon + SEGS - 7 * k - i, SEGS)).start()

        send(lax.rem(lon + SEGS // 2, SEGS)).start()

    spread(send_line)
    recv[lon] = msg[lon]

    def send_ext(l):
        d = l * PER + lat * (PER - 1)
        return d, remote(ext.at[l], ext_got.at[lon], x_s.at[l], x_r, at(d))

    for l in range(LEV):
        d, c = send_ext(l)

        @pl.when(d != lon)
        def _():
            c.start()

        @pl.when(d == lon)
        def _():
            ext_got[lon] = ext[l]

    for c in others:
        c.wait()
    for i, c in enumerate(smalls):
        if i != 2:
            c.wait()
    own = pl.multiple_of(lat * 128, 128)
    mid_w[...] = jnp.zeros_like(mid_w)
    mid_e[...] = jnp.zeros_like(mid_e)
    parts = ((fm, f, 0, 3), (um, u, 3, 2), (vm, v, 5, 2))
    for l in range(LEV):
        for ref, src, a, n in parts:
            mid_w[l, a : a + n] = src[l, 0:n, pl.ds(mid0, MW - 128)]
            mid_e[l, a : a + n] = src[l, SEG - n : SEG, pl.ds(mid0, MW - 128)]

    @pl.loop(0, LEV)
    def _(l):
        for ref, src, a, n in parts:
            ref[l, 3 : 3 + SEG, pl.ds(own, MW - 128)] = src[l, :, pl.ds(mid0, MW - 128)]

    mids = [
        remote(mid_w, mgot_e, ms.at[0], mr.at[0], west_dev),
        remote(mid_e, mgot_w, ms.at[1], mr.at[1], east_dev),
    ]
    src0 = pl.multiple_of((1 - lat) * (MW - 256) + lat * 128, 128)
    dst0 = pl.multiple_of(lat * (MW - 128), 128)
    lats = [
        remote(ref.at[:, :, pl.ds(src0, 128)], ref.at[:, :, pl.ds(dst0, 128)], ls.at[i], lr.at[i], partner)
        for i, ref in enumerate((fm, um, vm))
    ]

    def total(sem, ref, n):
        pltpu.make_async_copy(ref.at[pl.ds(0, n)], ref.at[pl.ds(0, n)], sem).wait()

    total(a_s, msg, SEGS - 1)
    for c in mids:
        c.start()
    total(a_r, recv, SEGS - 1)
    tt[:, SEG:C8] = jnp.zeros((WIN, C8 - SEG, 128), F32)
    uu[:, SEG:C8] = jnp.zeros((WIN, C8 - SEG, 128), F32)
    vv[:, SEG:C8] = jnp.zeros((WIN, C8 - SEG, 128), F32)
    for t in range(WIN):
        w = recv[:, t, :].T
        tt[t, 0:SEG] = w[0:SEG]
        uu[t, 0:SEG] = w[SEG : 2 * SEG]
        vv[t, 0 : SEG - TAIL] = w[2 * SEG : 128]
        if t == 0:
            sp[0] = w
        if t == WIN - 1:
            sp[1] = w

    @pl.when(jnp.logical_or(north_pole, south_pole))
    def _():
        total(x_r, ext_got, SEGS - 1)

    sp[2] = jnp.zeros((128, 128), F32)

    @pl.when(north_pole)
    def _():
        sp[0] = ext_got[:, 0, :].T
        sp[2] = ext_got[:, 1, :].T

    @pl.when(south_pole)
    def _():
        sp[1] = ext_got[:, 1, :].T
        sp[2] = ext_got[:, 0, :].T

    for i in range(8):
        t0 = i + 1 if i < 7 else 15
        t15 = i + 8 if i < 7 else 0
        lo, hi = SEG + TAIL * i, SEG + TAIL * (i + 1)
        vv[t0, SEG - TAIL : SEG] = sp[0, lo:hi]
        vv[t15, SEG - TAIL : SEG] = sp[1, lo:hi]

    e_in = pltpu.roll(sp[0, COLS - 5 : COLS + 19], 127, 1)
    w_in = pltpu.roll(sp[1, COLS - 5 : COLS + 19], 1, 1)
    for t in range(WIN):
        sw = rows_s[lat, CHUNK * jj + t]
        if t in (0, WIN - 1):
            u0 = sp[t // (WIN - 1), COLS + WIN : COLS + WIN + 1]
            u44 = sp[t // (WIN - 1), COLS + WIN + 1 : COLS + WIN + 2]
        else:
            u0, u44 = uu[t, 0:1], uu[t, SEG - 1 : SEG]
        r = 5 + 15 - t
        tt[t, SEG - 1 : SEG] += (0.02 * sw - 0.05 * sw * u44) * e_in[r : r + 1]
        tt[t, 0:1] += (0.02 * sw + 0.05 * sw * u0) * w_in[r : r + 1]
    opp = 0.05 * pltpu.roll(sp[2, 0:C8], SEGS // 2, 1)[:SEG]
    tt[0, 0:SEG] -= jnp.where(north_pole, vv[0, 0:SEG] * opp, 0.0)
    tt[WIN - 1, 0:SEG] += jnp.where(south_pole, vv[WIN - 1, 0:SEG] * opp, 0.0)

    col = lax.broadcasted_iota(jnp.int32, (C8, 128), 0)
    m_lane = lax.rem(lax.broadcasted_iota(jnp.int32, (1, KMAX), 1), KMAX // 2)
    o_lane = jnp.where(m_lane == 0, KMAX // 2, KMAX - m_lane)
    w_m = jnp.where(m_lane == 0, 1.0 / (SEG * SEGS), 2.0 / (SEG * SEGS))
    w_o = 2.0 / (SEG * SEGS)

    def lap(old, t):
        g = old[t]
        g8 = pltpu.roll(g[0:8], 127, 1)
        g40 = pltpu.roll(g[40:48], 1, 1)
        e = jnp.where(col == SEG - 1, jnp.broadcast_to(g8[0:1], (C8, 128)), pltpu.roll(g, C8 - 1, 0))
        w = jnp.where(col == 0, jnp.broadcast_to(g40[4:5], (C8, 128)), pltpu.roll(g, 1, 0))
        n = old[max(t - 1, 0)]
        s = old[min(t + 1, WIN - 1)]
        if t == 0:
            n = jnp.where(north_pole, pltpu.roll(g, SEGS // 2, 1), n)
        if t == WIN - 1:
            s = jnp.where(south_pole, pltpu.roll(g, SEGS // 2, 1), s)
        return tend(g, e, w, n, s, uu[t], vv[t], rows_s[lat, CHUNK * jj + t])

    def fold(z, table):
        p = jnp.sum(z * table, axis=0, keepdims=True)
        return p + pltpu.roll(p, KMAX // 2, 1)

    def substep(step, old, new, block):
        ts = range(BLOCK * block, BLOCK * (block + 1))
        raw = [tt[t] if step == 0 else tt[t] + lap(old, t) for t in ts]
        z = product(jnp.concatenate(raw, axis=0), fwd)
        modes = []
        for i, t in enumerate(ts):
            zt = z[C8 * i : C8 * (i + 1)]
            x = CHUNK * jj + t - 4 * lat
            cut = cuts[lat, jnp.minimum(jnp.maximum(x, 0), CAP - 1)]
            km = jnp.where(m_lane <= cut, w_m, 0.0)
            ko = jnp.where(o_lane <= cut, w_o, 0.0)
            modes.append(
                (fold(zt, twiddle[0]) * km) * twiddle[0]
                + (fold(zt, twiddle[1]) * km) * twiddle[1]
                + (fold(zt, twiddle[2]) * ko) * twiddle[2]
                + (fold(zt, twiddle[3]) * ko) * twiddle[3]
            )
        y = product(jnp.concatenate(modes, axis=0), inv)
        for i, t in enumerate(ts):
            x = CHUNK * jj + t - 4 * lat
            inside = jnp.logical_and(x >= 0, x < CAP)
            g = jnp.where(inside, y[C8 * i : C8 * (i + 1)], raw[i])
            new[t] = g if step == 0 else old[t] + g

    for step, (old, new) in enumerate(((gb, ga), (ga, gb), (gb, ga))):
        for block in range(WIN // BLOCK):
            substep(step, old, new, block)

    for i in range(CHUNK):
        st[SEG * i : SEG * (i + 1)] = ga[2 + i, 0:SEG]
    for i in range(2):
        st[SEG * (CHUNK + i) : SEG * (CHUNK + i + 1)] = jnp.where(lat == 0, ga[i, 0:SEG], ga[WIN - 2 + i, 0:SEG])
    st[SEG * (CHUNK + 2) :] = jnp.zeros((128 * RET - SEG * (CHUNK + 2), 128), F32)
    for p in range(RET):
        ret[:, p, :] = st[128 * p : 128 * (p + 1)].T

    def send_back(d):
        return remote(ret.at[d], back.at[lon], b_s, b_r.at[lon // PER], at(d))

    spread(send_back)
    back[lon] = ret[lon]
    for c in mids:
        c.wait()
    for l in range(LEV):
        for ref, src, a, n in parts:
            ref[l, 3 - n : 3, pl.ds(own, MW - 128)] = mgot_w[l, a : a + n]
            ref[l, 3 + SEG : 3 + SEG + n, pl.ds(own, MW - 128)] = mgot_e[l, a : a + n]
    for c in lats:
        c.start()

    for c in lats:
        c.wait()
    smid = mid_s[lat]

    @pl.loop(0, LEV)
    def _(l):
        for _ in range(3):
            x = fm[l]
            t = tend(
                x, pltpu.roll(x, 55, 0), pltpu.roll(x, 1, 0),
                pltpu.roll(x, 1, 1), pltpu.roll(x, MW - 1, 1), um[l], vm[l], smid,
            )
            fm[l] = x + t

    @pl.loop(0, LEV)
    def _(l):
        out[l, :, pl.ds(mid0, MW - 128)] = fm[l, 3 : 3 + SEG, pl.ds(own, MW - 128)]

    def store(l, first, lanes, half):
        return pltpu.make_async_copy(
            out.at[l, :, pl.ds(first, lanes)], out_hbm.at[:, l, pl.ds(first, lanes)], d_s.at[half, l]
        )

    stores = [store(l, rest0, ROWS - CW, 0) for l in range(LEV)]
    for c in stores:
        c.start()
    rl[:, CAP:CW] = jnp.zeros((LEV, CW - CAP, 128), F32)
    lane128 = lax.broadcasted_iota(jnp.int32, (PER, 128), 1)
    x = lane1 - lat * SHIFT
    inside = jnp.logical_and(x >= 2 * lat, x < CAP + 2 + 2 * lat)
    ends = []
    for order, step in enumerate((0, 1, 3, 2)):
        l = lax.rem(lon // PER + step, LEV)
        total(b_r.at[l], back, PER - 1 if order == 0 else PER)
        mine = back.at[pl.ds(pl.multiple_of(l * PER, PER), PER)]
        for i in range(CHUNK + 2):
            p, off = divmod(SEG * i, 128)
            r = mine[:, p, :]
            if off:
                r = pltpu.roll(r, 128 - off, 1)
            if off + SEG > 128:
                r = jnp.where(lane128 < 128 - off, r, pltpu.roll(mine[:, p + 1, :], 128 - off, 1))
            if i < CHUNK:
                rl[order, pl.ds(2 + i, PER, stride=CHUNK), :] = r
            else:
                rl[order, i - CHUNK : i - CHUNK + 1] = r[0:1]
                rl[order, CAP + 2 + i - CHUNK : CAP + 3 + i - CHUNK] = r[PER - 1 : PER]
        add = jnp.concatenate([rl[order, 128 * b : 128 * (b + 1)].T[0:C8] for b in range(CW // 128)], axis=1)
        add = pltpu.roll(add, lat * SHIFT, 1)[0:SEG]
        old = out[l, :, pl.ds(cap0, CW)]
        out[l, :, pl.ds(cap0, CW)] = jnp.where(inside, f[l, :, pl.ds(cap0, CW)] + add, old)
        ends.append(store(l, cap0, CW, 1))
        ends[-1].start()

    total(b_s, ret, SEGS - 1)
    for l in range(LEV):
        d, c = send_ext(l)

        @pl.when(d != lon)
        def _():
            c.wait_send()

    for c in stores + ends:
        c.wait()


def body(f, u, v, cutoffs):
    cap_s, mid_s, rows_s = stretch_table()
    small = (cutoffs, rows_s, cap_s, mid_s) + tables()
    V = lambda *shape: pltpu.VMEM(shape, F32)
    dma = pltpu.SemaphoreType.DMA
    f, u, v = (jnp.transpose(a, (1, 0, 2)) for a in (f, u, v))
    done = pl.pallas_call(
        kernel,
        out_shape=jax.ShapeDtypeStruct(f.shape, F32),
        in_specs=[pl.BlockSpec(memory_space=pl.ANY)] * (3 + SMALL),
        out_specs=pl.BlockSpec(memory_space=pl.ANY),
        scratch_shapes=[
            pltpu.SMEM(cutoffs.shape, jnp.int32), pltpu.SMEM(rows_s.shape, F32),
            V(*cap_s.shape), V(*mid_s.shape),
            pltpu.VMEM((256, 256), BF16), pltpu.VMEM((256, 256), BF16), V(4, C8, 128), dma((SMALL,)),
            V(LEV, SEG, ROWS), V(LEV, SEG, ROWS), V(LEV, SEG, ROWS), V(LEV, SEG, ROWS),
            V(LEV, 8, MW - 128), V(LEV, 8, MW - 128), V(LEV, 8, MW - 128), V(LEV, 8, MW - 128),
            V(LEV, 56, MW), V(LEV, 56, MW), V(LEV, 56, MW),
            V(136, CW), V(128, CW), V(CW, 128), V(CW, 128),
            V(SEGS, WIN, 128), V(SEGS, WIN, 128), V(LEV, 2, 128), V(SEGS, 2, 128), V(3, 128, 128),
            V(WIN, C8, 128), V(WIN, C8, 128), V(WIN, C8, 128), V(WIN, C8, 128), V(WIN, C8, 128),
            V(128 * RET, 128), V(SEGS, RET, 128), V(SEGS, RET, 128), V(LEV, CW, 128),
            dma((2, LEV)), dma((3, LEV)), dma((3, LEV)), dma((2,)), dma((2,)), dma((3,)), dma((3,)),
            dma, dma, dma((LEV,)), dma, dma, dma((LEV,)),
        ],
        compiler_params=pltpu.CompilerParams(
            collective_id=0, has_side_effects=True, vmem_limit_bytes=60 * 1024 * 1024
        ),
    )(f, u, v, *small)
    return jnp.transpose(done, (1, 0, 2))


def solution(mesh):
    placed = (P(None, "lon", "lat"), P(None, "lon", "lat"), P(None, "lon", "lat"), P())
    return jax.shard_map(
        body, mesh=mesh, in_specs=placed, out_specs=P(None, "lon", "lat"), check_vma=False
    )
```

```python
import functools
import math

import jax
import jax.numpy as jnp
import ml_dtypes
import numpy as np
from jax import lax
from jax.experimental import pallas as pl
from jax.experimental.pallas import tpu as pltpu
from jax.sharding import PartitionSpec as P

MESH = pl.DeviceIdType.MESH
LEV, SEG, ROWS, SEGS = 4, 45, 1152, 128
CAP = ROWS // 3
CHUNK, WIN = 12, 16
PER = CAP // CHUNK
CW = 512
SHIFT = CW - CAP - 4
MW = 1024
KMAX = 128
C8 = 48
BLOCK = 16
RET = 5
SMALL = 7
COLS = 101
TAIL = 7
F32, BF16 = jnp.float32, jnp.bfloat16


def split(x):
    hi = x.astype(ml_dtypes.bfloat16)
    return hi, (x - hi.astype(np.float32)).astype(ml_dtypes.bfloat16)


def two_parts(basis):
    hi, lo = split(np.ascontiguousarray(basis))
    return np.concatenate(
        [np.concatenate([hi, lo], axis=1), np.concatenate([hi, np.zeros_like(lo)], axis=1)], axis=0
    )


def tables():
    total = SEG * SEGS
    half = KMAX // 2
    m, s, c = np.arange(half), np.arange(SEGS), np.arange(SEG)
    a = 2 * np.pi * ((s[:, None] * m[None, :]) % SEGS) / SEGS
    sin = np.sin(a)
    sin[:, 0] = np.where(s % 2 == 0, 1.0, -1.0)
    basis = np.concatenate([np.cos(a), sin], axis=1).astype(np.float32)
    other = np.where(m == 0, half, KMAX - m)
    angle = lambda k: 2 * np.pi * (c[:, None] * k[None, :]) / total
    cm, sm, co, so = np.cos(angle(m)), np.sin(angle(m)), np.cos(angle(other)), np.sin(angle(other))
    ta, tb = np.concatenate([cm, -sm], axis=1), np.concatenate([sm, cm], axis=1)
    pa, pb = np.concatenate([co, so], axis=1), np.concatenate([so, -co], axis=1)
    ta[:, half], tb[:, half], pa[:, 0], pb[:, 0] = 0.0, 0.0, 0.0, 0.0
    pa[:, half], pb[:, half] = co[:, 0], so[:, 0]
    twiddle = np.pad(np.stack([ta, tb, pa, pb]), ((0, 0), (0, C8 - SEG), (0, 0))).astype(np.float32)
    return two_parts(basis), two_parts(basis.T), twiddle


def stretch_table():
    colat = np.float32(math.pi) * (np.arange(2 * ROWS).astype(np.float32) + np.float32(0.5))
    colat = (colat / np.float32(2 * ROWS)).astype(np.float32)
    s = np.float32(1.0) / np.maximum(np.sin(colat), np.float32(0.125))
    s = np.pad(s.astype(np.float32), (0, MW))
    cap = np.stack([s[:CW], s[2 * ROWS - CW : 2 * ROWS]])[:, None, :]
    mid = np.stack([s[256 : 256 + MW], s[ROWS - 128 : ROWS - 128 + MW]])[:, None, :]
    rows = np.stack([s[: CAP + 4], s[2 * ROWS - CAP - 4 : 2 * ROWS]])
    return cap, mid, rows


def tend(mid, east, west, north, south, u, v, s):
    return (
        -0.05 * s * u * (east - west)
        - 0.05 * v * (north - south)
        + 0.02 * s * (east - 2.0 * mid + west)
    )


def product(x, parts_ref):
    hi = x.astype(BF16)
    lo = (x - hi.astype(F32)).astype(BF16)
    r = jnp.dot(jnp.concatenate([hi, lo], axis=1), parts_ref[...], preferred_element_type=F32)
    return r[:, 0:128] + r[:, 128:]


def kernel(
    f_hbm, u_hbm, v_hbm, *rest,
):
    small, (out_hbm, *scratch) = rest[:SMALL], rest[SMALL:]
    run(f_hbm, u_hbm, v_hbm, small, out_hbm, *scratch)


def run(
    f_hbm, u_hbm, v_hbm, small, out_hbm,
    cuts, rows_s, cap_s, mid_s, fwd, inv, twiddle, small_s,
    out, f, u, v, mid_w, mid_e, mgot_w, mgot_e,
    fm, um, vm, mm, mx, ln, lx, msg, recv, ext, ext_got, sp,
    tt, uu, vv, ga, gb, st, ret, back, rl,
    d_s, cs, os, ms, mr, ls, lr, a_s, a_r, x_s, x_r, b_s, b_r,
):
    lat = lax.axis_index("lat")
    lon = lax.axis_index("lon")
    south = lat == 1
    jj = lax.rem(lon, PER)
    north_pole = jnp.logical_and(lat == 0, jj == 0)
    south_pole = jnp.logical_and(lat == 1, jj == PER - 1)
    at = lambda d: (lat, d)
    east_dev = at(lax.rem(lon + 1, SEGS))
    west_dev = at(lax.rem(lon + SEGS - 1, SEGS))
    partner = (1 - lat, lon)

    cap0 = pl.multiple_of(lat * (ROWS - CW), 128)
    mid0 = pl.multiple_of((1 - lat) * 256, 128)
    rest0 = pl.multiple_of((1 - lat) * CW, 128)
    pairs = ((f_hbm, f), (u_hbm, u), (v_hbm, v))

    def load(i, l, first, lanes, sems):
        src, dst = pairs[i]
        return pltpu.make_async_copy(
            src.at[:, l, pl.ds(first, lanes)], dst.at[l, :, pl.ds(first, lanes)], sems.at[i, l]
        )

    others = [load(i, l, rest0, ROWS - CW, os) for l in range(LEV) for i in range(3)]
    barrier = pltpu.get_barrier_semaphore()

    def greet(k):
        pl.semaphore_signal(barrier, inc=1, device_id=at(lax.rem(lon + k, SEGS)), device_id_type=MESH)

    @pl.loop(0, (SEGS - 1) // 8)
    def _(k):
        for i in range(8):
            greet(8 * k + i + 1)

    for k in range((SEGS - 1) // 8 * 8 + 1, SEGS):
        greet(k)
    pl.semaphore_signal(barrier, inc=1, device_id=partner, device_id_type=MESH)

    held = (cuts, rows_s, cap_s, mid_s, fwd, inv, twiddle)
    smalls = [pltpu.make_async_copy(src, dst, small_s.at[i]) for i, (src, dst) in enumerate(zip(small, held))]
    for l in range(LEV):
        for i in range(3):
            load(i, l, cap0, CW, cs).start()
        if l == 0:
            smalls[2].start()
    for i, c in enumerate(smalls):
        if i != 2:
            c.start()
    for c in others:
        c.start()
    smalls[2].wait()

    lanes = lax.broadcasted_iota(jnp.int32, (C8, CW), 1)
    scap = cap_s[lat]
    row = lax.broadcasted_iota(jnp.int32, (WIN, 128), 0)
    lane1 = lanes[:SEG]
    pole = jnp.where(lat == 0, 0, CW - 1)

    @pl.loop(0, LEV)
    def _(l):
        for i in range(3):
            load(i, l, cap0, CW, cs).wait()
        fc = f[l, :, pl.ds(cap0, CW)]
        uc = u[l, :, pl.ds(cap0, CW)]
        vc = v[l, :, pl.ds(cap0, CW)]
        zero = jnp.zeros((1, CW), F32)
        e = jnp.concatenate([fc[1:], zero], axis=0)
        w = jnp.concatenate([zero, fc[:-1]], axis=0)
        n = jnp.where(jnp.logical_and(lane1 == pole, lat == 0), 0.0, pltpu.roll(fc, 1, 1))
        s = jnp.where(jnp.logical_and(lane1 == pole, lat == 1), 0.0, pltpu.roll(fc, CW - 1, 1))
        turn = lax.rem(CW - lat * SHIFT, CW)
        mm[0:SEG] = pltpu.roll(tend(fc, e, w, n, s, uc, vc, scap), turn, 1)
        mm[SEG : 2 * SEG] = pltpu.roll(uc, turn, 1)
        mm[2 * SEG : 3 * SEG] = pltpu.roll(vc, turn, 1)
        vt = mm[128 : 128 + TAIL]
        x12 = lax.rem(lanes[:WIN], 12)
        edge = pltpu.roll(fc, lax.rem(CW - lat * (SHIFT + 2) + 1, CW), 1)
        mx[0:SEG] = jnp.where(lane1 == jnp.where(lat == 0, 1, CAP + 2), edge, mm[0:SEG])
        for i in range(8):
            t0 = i + 1 if i < 7 else 15
            t15 = i + 8 if i < 7 else 0
            a0 = pltpu.roll(vt, CW - t0, 1)
            a15 = pltpu.roll(vt, 15 - t15, 1)
            mx[SEG + TAIL * i : SEG + TAIL * (i + 1)] = jnp.where(x12[:TAIL] == 3, a15, a0)
        ft = pltpu.roll(fc, turn, 1)
        f0 = jnp.broadcast_to(ft[0:1], (WIN, CW))
        f44 = jnp.broadcast_to(ft[SEG - 1 : SEG], (WIN, CW))
        f0 = pltpu.roll(f0, CW - 15, 1, stride=1, stride_axis=0)
        f44 = pltpu.roll(f44, 0, 1, stride=1, stride_axis=0)
        mx[COLS : COLS + WIN] = jnp.where(x12 == 3, f44, f0)
        mx[COLS + WIN : COLS + WIN + 1] = mm[SEG : SEG + 1]
        mx[COLS + WIN + 1 : COLS + WIN + 2] = mm[2 * SEG - 1 : 2 * SEG]
        for b in range(CW // 128):
            ln[128 * b : 128 * (b + 1)] = mm[0:128, 128 * b : 128 * (b + 1)].T
            lx[128 * b : 128 * (b + 1)] = mx[0:128, 128 * b : 128 * (b + 1)].T

        @pl.loop(0, PER // 8)
        def _(mo):
            for mi in range(4):
                m = 4 * mo + mi
                a = ln[pl.ds(pl.multiple_of(24 * m, 8), 32)]
                b = lx[pl.ds(pl.multiple_of(24 * m, 8), 32)]
                first = jnp.logical_and(m == 0, lat == 0)
                last = jnp.logical_and(m == PER // 2 - 1, lat == 1)
                use0 = jnp.logical_or(jnp.logical_and(row == 0, jnp.logical_not(first)), row == WIN - 1)
                use1 = jnp.logical_or(row == 0, jnp.logical_and(row == WIN - 1, jnp.logical_not(last)))
                msg[l * PER + 2 * m] = jnp.where(use0, b[0:16], a[0:16])
                msg[l * PER + 2 * m + 1] = jnp.where(use1, b[12:28], a[12:28])

        ext[l] = jnp.where(lat == 0, lx[0:2], lx[CAP + 2 : CAP + 4])

    pl.semaphore_wait(barrier, SEGS)

    def remote(src, dst, send, recv_sem, dev):
        return pltpu.make_async_remote_copy(
            src_ref=src, dst_ref=dst, send_sem=send, recv_sem=recv_sem,
            device_id=dev, device_id_type=MESH,
        )

    def send_line(d):
        return remote(msg.at[d], recv.at[lon], a_s, a_r, at(d))

    def spread(send):
        @pl.loop(0, (SEGS // 2 - 1) // 7)
        def _(k):
            for i in range(1, 8):
                send(lax.rem(lon + 7 * k + i, SEGS)).start()
                send(lax.rem(lon + SEGS - 7 * k - i, SEGS)).start()

        send(lax.rem(lon + SEGS // 2, SEGS)).start()

    def send_ext(l):
        d = l * PER + lat * (PER - 1)
        return d, remote(ext.at[l], ext_got.at[lon], x_s.at[l], x_r, at(d))

    for l in range(LEV):
        d, c = send_ext(l)

        @pl.when(d != lon)
        def _():
            c.start()

        @pl.when(d == lon)
        def _():
            ext_got[lon] = ext[l]

    spread(send_line)
    recv[lon] = msg[lon]

    for c in others:
        c.wait()
    for i, c in enumerate(smalls):
        if i != 2:
            c.wait()
    own = pl.multiple_of(lat * 128, 128)
    mid_w[...] = jnp.zeros_like(mid_w)
    mid_e[...] = jnp.zeros_like(mid_e)
    parts = ((fm, f, 0, 3), (um, u, 3, 2), (vm, v, 5, 2))
    for l in range(LEV):
        for ref, src, a, n in parts:
            mid_w[l, a : a + n] = src[l, 0:n, pl.ds(mid0, MW - 128)]
            mid_e[l, a : a + n] = src[l, SEG - n : SEG, pl.ds(mid0, MW - 128)]

    @pl.loop(0, LEV)
    def _(l):
        for ref, src, a, n in parts:
            ref[l, 3 : 3 + SEG, pl.ds(own, MW - 128)] = src[l, :, pl.ds(mid0, MW - 128)]

    mids = [
        remote(mid_w, mgot_e, ms.at[0], mr.at[0], west_dev),
        remote(mid_e, mgot_w, ms.at[1], mr.at[1], east_dev),
    ]
    src0 = pl.multiple_of((1 - lat) * (MW - 256) + lat * 128, 128)
    dst0 = pl.multiple_of(lat * (MW - 128), 128)
    lats = [
        remote(ref.at[:, :, pl.ds(src0, 128)], ref.at[:, :, pl.ds(dst0, 128)], ls.at[i], lr.at[i], partner)
        for i, ref in enumerate((fm, um, vm))
    ]

    def total(sem, ref, n):
        pltpu.make_async_copy(ref.at[pl.ds(0, n)], ref.at[pl.ds(0, n)], sem).wait()

    total(a_s, msg, SEGS - 1)
    for c in mids:
        c.start()
    total(a_r, recv, SEGS - 1)
    tt[:, SEG:C8] = jnp.zeros((WIN, C8 - SEG, 128), F32)
    uu[:, SEG:C8] = jnp.zeros((WIN, C8 - SEG, 128), F32)
    vv[:, SEG:C8] = jnp.zeros((WIN, C8 - SEG, 128), F32)
    for t in range(WIN):
        w = recv[:, t, :].T
        tt[t, 0:SEG] = w[0:SEG]
        uu[t, 0:SEG] = w[SEG : 2 * SEG]
        vv[t, 0 : SEG - TAIL] = w[2 * SEG : 128]
        if t == 0:
            sp[0] = w
        if t == WIN - 1:
            sp[1] = w

    @pl.when(jnp.logical_or(north_pole, south_pole))
    def _():
        total(x_r, ext_got, SEGS - 1)

    sp[2] = jnp.zeros((128, 128), F32)

    @pl.when(north_pole)
    def _():
        sp[0] = ext_got[:, 0, :].T
        sp[2] = ext_got[:, 1, :].T

    @pl.when(south_pole)
    def _():
        sp[1] = ext_got[:, 1, :].T
        sp[2] = ext_got[:, 0, :].T

    for i in range(8):
        t0 = i + 1 if i < 7 else 15
        t15 = i + 8 if i < 7 else 0
        lo, hi = SEG + TAIL * i, SEG + TAIL * (i + 1)
        vv[t0, SEG - TAIL : SEG] = sp[0, lo:hi]
        vv[t15, SEG - TAIL : SEG] = sp[1, lo:hi]

    e_in = pltpu.roll(sp[0, COLS - 5 : COLS + 19], 127, 1)
    w_in = pltpu.roll(sp[1, COLS - 5 : COLS + 19], 1, 1)
    for t in range(WIN):
        sw = rows_s[lat, CHUNK * jj + t]
        if t in (0, WIN - 1):
            u0 = sp[t // (WIN - 1), COLS + WIN : COLS + WIN + 1]
            u44 = sp[t // (WIN - 1), COLS + WIN + 1 : COLS + WIN + 2]
        else:
            u0, u44 = uu[t, 0:1], uu[t, SEG - 1 : SEG]
        r = 5 + 15 - t
        tt[t, SEG - 1 : SEG] += (0.02 * sw - 0.05 * sw * u44) * e_in[r : r + 1]
        tt[t, 0:1] += (0.02 * sw + 0.05 * sw * u0) * w_in[r : r + 1]
    opp = 0.05 * pltpu.roll(sp[2, 0:C8], SEGS // 2, 1)[:SEG]
    tt[0, 0:SEG] -= jnp.where(north_pole, vv[0, 0:SEG] * opp, 0.0)
    tt[WIN - 1, 0:SEG] += jnp.where(south_pole, vv[WIN - 1, 0:SEG] * opp, 0.0)

    col = lax.broadcasted_iota(jnp.int32, (C8, 128), 0)
    m_lane = lax.rem(lax.broadcasted_iota(jnp.int32, (1, KMAX), 1), KMAX // 2)
    o_lane = jnp.where(m_lane == 0, KMAX // 2, KMAX - m_lane)
    w_m = jnp.where(m_lane == 0, 1.0 / (SEG * SEGS), 2.0 / (SEG * SEGS))
    w_o = 2.0 / (SEG * SEGS)

    def lap(old, t):
        g = old[t]
        g8 = pltpu.roll(g[0:8], 127, 1)
        g40 = pltpu.roll(g[40:48], 1, 1)
        e = jnp.where(col == SEG - 1, jnp.broadcast_to(g8[0:1], (C8, 128)), pltpu.roll(g, C8 - 1, 0))
        w = jnp.where(col == 0, jnp.broadcast_to(g40[4:5], (C8, 128)), pltpu.roll(g, 1, 0))
        n = old[max(t - 1, 0)]
        s = old[min(t + 1, WIN - 1)]
        if t == 0:
            n = jnp.where(north_pole, pltpu.roll(g, SEGS // 2, 1), n)
        if t == WIN - 1:
            s = jnp.where(south_pole, pltpu.roll(g, SEGS // 2, 1), s)
        return tend(g, e, w, n, s, uu[t], vv[t], rows_s[lat, CHUNK * jj + t])

    def fold(z, table):
        p = jnp.sum(z * table, axis=0, keepdims=True)
        return p + pltpu.roll(p, KMAX // 2, 1)

    def substep(step, old, new, block):
        ts = range(BLOCK * block, BLOCK * (block + 1))
        raw = [tt[t] if step == 0 else tt[t] + lap(old, t) for t in ts]
        z = product(jnp.concatenate(raw, axis=0), fwd)
        modes = []
        for i, t in enumerate(ts):
            zt = z[C8 * i : C8 * (i + 1)]
            x = CHUNK * jj + t - 4 * lat
            cut = cuts[lat, jnp.minimum(jnp.maximum(x, 0), CAP - 1)]
            km = jnp.where(m_lane <= cut, w_m, 0.0)
            ko = jnp.where(o_lane <= cut, w_o, 0.0)
            modes.append(
                (fold(zt, twiddle[0]) * km) * twiddle[0]
                + (fold(zt, twiddle[1]) * km) * twiddle[1]
                + (fold(zt, twiddle[2]) * ko) * twiddle[2]
                + (fold(zt, twiddle[3]) * ko) * twiddle[3]
            )
        y = product(jnp.concatenate(modes, axis=0), inv)
        for i, t in enumerate(ts):
            x = CHUNK * jj + t - 4 * lat
            inside = jnp.logical_and(x >= 0, x < CAP)
            g = jnp.where(inside, y[C8 * i : C8 * (i + 1)], raw[i])
            new[t] = g if step == 0 else old[t] + g

    for step, (old, new) in enumerate(((gb, ga), (ga, gb), (gb, ga))):
        for block in range(WIN // BLOCK):
            substep(step, old, new, block)

    for i in range(CHUNK):
        st[SEG * i : SEG * (i + 1)] = ga[2 + i, 0:SEG]
    for i in range(2):
        st[SEG * (CHUNK + i) : SEG * (CHUNK + i + 1)] = jnp.where(lat == 0, ga[i, 0:SEG], ga[WIN - 2 + i, 0:SEG])
    st[SEG * (CHUNK + 2) :] = jnp.zeros((128 * RET - SEG * (CHUNK + 2), 128), F32)
    for p in range(RET):
        ret[:, p, :] = st[128 * p : 128 * (p + 1)].T

    def send_back(d):
        return remote(ret.at[d], back.at[lon], b_s, b_r.at[lon // PER], at(d))

    spread(send_back)
    back[lon] = ret[lon]
    for c in mids:
        c.wait()
    for l in range(LEV):
        for ref, src, a, n in parts:
            ref[l, 3 - n : 3, pl.ds(own, MW - 128)] = mgot_w[l, a : a + n]
            ref[l, 3 + SEG : 3 + SEG + n, pl.ds(own, MW - 128)] = mgot_e[l, a : a + n]
    for c in lats:
        c.start()

    for c in lats:
        c.wait()
    smid = mid_s[lat]

    @pl.loop(0, LEV)
    def _(l):
        for _ in range(3):
            x = fm[l]
            t = tend(
                x, pltpu.roll(x, 55, 0), pltpu.roll(x, 1, 0),
                pltpu.roll(x, 1, 1), pltpu.roll(x, MW - 1, 1), um[l], vm[l], smid,
            )
            fm[l] = x + t

    @pl.loop(0, LEV)
    def _(l):
        out[l, :, pl.ds(mid0, MW - 128)] = fm[l, 3 : 3 + SEG, pl.ds(own, MW - 128)]

    def store(l, first, lanes, half):
        return pltpu.make_async_copy(
            out.at[l, :, pl.ds(first, lanes)], out_hbm.at[:, l, pl.ds(first, lanes)], d_s.at[half, l]
        )

    stores = [store(l, rest0, ROWS - CW, 0) for l in range(LEV)]
    for c in stores:
        c.start()
    rl[:, CAP:CW] = jnp.zeros((LEV, CW - CAP, 128), F32)
    lane128 = lax.broadcasted_iota(jnp.int32, (PER, 128), 1)
    x = lane1 - lat * SHIFT
    inside = jnp.logical_and(x >= 2 * lat, x < CAP + 2 + 2 * lat)
    ends = []
    for order, step in enumerate((0, 1, 3, 2)):
        l = lax.rem(lon // PER + step, LEV)
        total(b_r.at[l], back, PER - 1 if order == 0 else PER)
        mine = back.at[pl.ds(pl.multiple_of(l * PER, PER), PER)]
        for i in range(CHUNK + 2):
            p, off = divmod(SEG * i, 128)
            r = mine[:, p, :]
            if off:
                r = pltpu.roll(r, 128 - off, 1)
            if off + SEG > 128:
                r = jnp.where(lane128 < 128 - off, r, pltpu.roll(mine[:, p + 1, :], 128 - off, 1))
            if i < CHUNK:
                rl[order, pl.ds(2 + i, PER, stride=CHUNK), :] = r
            else:
                rl[order, i - CHUNK : i - CHUNK + 1] = r[0:1]
                rl[order, CAP + 2 + i - CHUNK : CAP + 3 + i - CHUNK] = r[PER - 1 : PER]
        add = jnp.concatenate([rl[order, 128 * b : 128 * (b + 1)].T[0:C8] for b in range(CW // 128)], axis=1)
        add = pltpu.roll(add, lat * SHIFT, 1)[0:SEG]
        old = out[l, :, pl.ds(cap0, CW)]
        out[l, :, pl.ds(cap0, CW)] = jnp.where(inside, f[l, :, pl.ds(cap0, CW)] + add, old)
        ends.append(store(l, cap0, CW, 1))
        ends[-1].start()

    total(b_s, ret, SEGS - 1)
    for l in range(LEV):
        d, c = send_ext(l)

        @pl.when(d != lon)
        def _():
            c.wait_send()

    for c in stores + ends:
        c.wait()


def body(f, u, v, cutoffs):
    cap_s, mid_s, rows_s = stretch_table()
    small = (cutoffs, rows_s, cap_s, mid_s) + tables()
    V = lambda *shape: pltpu.VMEM(shape, F32)
    dma = pltpu.SemaphoreType.DMA
    f, u, v = (jnp.transpose(a, (1, 0, 2)) for a in (f, u, v))
    done = pl.pallas_call(
        kernel,
        out_shape=jax.ShapeDtypeStruct(f.shape, F32),
        in_specs=[pl.BlockSpec(memory_space=pl.ANY)] * (3 + SMALL),
        out_specs=pl.BlockSpec(memory_space=pl.ANY),
        scratch_shapes=[
            pltpu.SMEM(cutoffs.shape, jnp.int32), pltpu.SMEM(rows_s.shape, F32),
            V(*cap_s.shape), V(*mid_s.shape),
            pltpu.VMEM((256, 256), BF16), pltpu.VMEM((256, 256), BF16), V(4, C8, 128), dma((SMALL,)),
            V(LEV, SEG, ROWS), V(LEV, SEG, ROWS), V(LEV, SEG, ROWS), V(LEV, SEG, ROWS),
            V(LEV, 8, MW - 128), V(LEV, 8, MW - 128), V(LEV, 8, MW - 128), V(LEV, 8, MW - 128),
            V(LEV, 56, MW), V(LEV, 56, MW), V(LEV, 56, MW),
            V(136, CW), V(128, CW), V(CW, 128), V(CW, 128),
            V(SEGS, WIN, 128), V(SEGS, WIN, 128), V(LEV, 2, 128), V(SEGS, 2, 128), V(3, 128, 128),
            V(WIN, C8, 128), V(WIN, C8, 128), V(WIN, C8, 128), V(WIN, C8, 128), V(WIN, C8, 128),
            V(128 * RET, 128), V(SEGS, RET, 128), V(SEGS, RET, 128), V(LEV, CW, 128),
            dma((2, LEV)), dma((3, LEV)), dma((3, LEV)), dma((2,)), dma((2,)), dma((3,)), dma((3,)),
            dma, dma, dma((LEV,)), dma, dma, dma((LEV,)),
        ],
        compiler_params=pltpu.CompilerParams(
            collective_id=0, has_side_effects=True, vmem_limit_bytes=60 * 1024 * 1024
        ),
    )(f, u, v, *small)
    return jnp.transpose(done, (1, 0, 2))


def solution(mesh):
    placed = (P(None, "lon", "lat"), P(None, "lon", "lat"), P(None, "lon", "lat"), P())
    return jax.shard_map(
        body, mesh=mesh, in_specs=placed, out_specs=P(None, "lon", "lat"), check_vma=False
    )
```

```python
import functools
import math

import jax
import jax.numpy as jnp
import ml_dtypes
import numpy as np
from jax import lax
from jax.experimental import pallas as pl
from jax.experimental.pallas import tpu as pltpu
from jax.sharding import PartitionSpec as P

MESH = pl.DeviceIdType.MESH
LEV, SEG, ROWS, SEGS = 4, 45, 1152, 128
CAP = ROWS // 3
CHUNK, WIN = 12, 16
PER = CAP // CHUNK
CW = 512
SHIFT = CW - CAP - 4
MW = 1024
KMAX = 128
C8 = 48
BLOCK = 16
RET = 5
SMALL = 7
COLS = 101
TAIL = 7
F32, BF16 = jnp.float32, jnp.bfloat16


def split(x):
    hi = x.astype(ml_dtypes.bfloat16)
    return hi, (x - hi.astype(np.float32)).astype(ml_dtypes.bfloat16)


def two_parts(basis):
    hi, lo = split(np.ascontiguousarray(basis))
    return np.concatenate(
        [np.concatenate([hi, lo], axis=1), np.concatenate([hi, np.zeros_like(lo)], axis=1)], axis=0
    )


def tables():
    total = SEG * SEGS
    half = KMAX // 2
    m, s, c = np.arange(half), np.arange(SEGS), np.arange(SEG)
    a = 2 * np.pi * ((s[:, None] * m[None, :]) % SEGS) / SEGS
    sin = np.sin(a)
    sin[:, 0] = np.where(s % 2 == 0, 1.0, -1.0)
    basis = np.concatenate([np.cos(a), sin], axis=1).astype(np.float32)
    other = np.where(m == 0, half, KMAX - m)
    angle = lambda k: 2 * np.pi * (c[:, None] * k[None, :]) / total
    cm, sm, co, so = np.cos(angle(m)), np.sin(angle(m)), np.cos(angle(other)), np.sin(angle(other))
    ta, tb = np.concatenate([cm, -sm], axis=1), np.concatenate([sm, cm], axis=1)
    pa, pb = np.concatenate([co, so], axis=1), np.concatenate([so, -co], axis=1)
    ta[:, half], tb[:, half], pa[:, 0], pb[:, 0] = 0.0, 0.0, 0.0, 0.0
    pa[:, half], pb[:, half] = co[:, 0], so[:, 0]
    twiddle = np.pad(np.stack([ta, tb, pa, pb]), ((0, 0), (0, C8 - SEG), (0, 0))).astype(np.float32)
    return two_parts(basis), two_parts(basis.T), twiddle


def stretch_table():
    colat = np.float32(math.pi) * (np.arange(2 * ROWS).astype(np.float32) + np.float32(0.5))
    colat = (colat / np.float32(2 * ROWS)).astype(np.float32)
    s = np.float32(1.0) / np.maximum(np.sin(colat), np.float32(0.125))
    s = np.pad(s.astype(np.float32), (0, MW))
    cap = np.stack([s[:CW], s[2 * ROWS - CW : 2 * ROWS]])[:, None, :]
    mid = np.stack([s[256 : 256 + MW], s[ROWS - 128 : ROWS - 128 + MW]])[:, None, :]
    rows = np.stack([s[: CAP + 4], s[2 * ROWS - CAP - 4 : 2 * ROWS]])
    return cap, mid, rows


def tend(mid, east, west, north, south, u, v, s):
    return (
        -0.05 * s * u * (east - west)
        - 0.05 * v * (north - south)
        + 0.02 * s * (east - 2.0 * mid + west)
    )


def product(x, parts_ref):
    hi = x.astype(BF16)
    lo = (x - hi.astype(F32)).astype(BF16)
    r = jnp.dot(jnp.concatenate([hi, lo], axis=1), parts_ref[...], preferred_element_type=F32)
    return r[:, 0:128] + r[:, 128:]


def kernel(
    f_hbm, u_hbm, v_hbm, *rest,
):
    small, (out_hbm, *scratch) = rest[:SMALL], rest[SMALL:]
    run(f_hbm, u_hbm, v_hbm, small, out_hbm, *scratch)


def run(
    f_hbm, u_hbm, v_hbm, small, out_hbm,
    cuts, rows_s, cap_s, mid_s, fwd, inv, twiddle, small_s,
    out, f, u, v, mid_w, mid_e, mgot_w, mgot_e,
    fm, um, vm, mm, mx, ln, lx, msg, recv, ext, ext_got, sp,
    tt, uu, vv, ga, gb, st, ret, back, rl,
    d_s, cs, os, ms, mr, ls, lr, a_s, a_r, x_s, x_r, b_s, b_r,
):
    lat = lax.axis_index("lat")
    lon = lax.axis_index("lon")
    south = lat == 1
    jj = lax.rem(lon, PER)
    north_pole = jnp.logical_and(lat == 0, jj == 0)
    south_pole = jnp.logical_and(lat == 1, jj == PER - 1)
    at = lambda d: (lat, d)
    east_dev = at(lax.rem(lon + 1, SEGS))
    west_dev = at(lax.rem(lon + SEGS - 1, SEGS))
    partner = (1 - lat, lon)

    cap0 = pl.multiple_of(lat * (ROWS - CW), 128)
    mid0 = pl.multiple_of((1 - lat) * 256, 128)
    rest0 = pl.multiple_of((1 - lat) * CW, 128)
    pairs = ((f_hbm, f), (u_hbm, u), (v_hbm, v))

    def load(i, l, first, lanes, sems):
        src, dst = pairs[i]
        return pltpu.make_async_copy(
            src.at[:, l, pl.ds(first, lanes)], dst.at[l, :, pl.ds(first, lanes)], sems.at[i, l]
        )

    others = [load(i, l, rest0, ROWS - CW, os) for l in range(LEV) for i in range(3)]
    barrier = pltpu.get_barrier_semaphore()

    def greet(k):
        pl.semaphore_signal(barrier, inc=1, device_id=at(lax.rem(lon + k, SEGS)), device_id_type=MESH)

    @pl.loop(0, (SEGS - 1) // 8)
    def _(k):
        for i in range(8):
            greet(8 * k + i + 1)

    for k in range((SEGS - 1) // 8 * 8 + 1, SEGS):
        greet(k)
    pl.semaphore_signal(barrier, inc=1, device_id=partner, device_id_type=MESH)

    held = (cuts, rows_s, cap_s, mid_s, fwd, inv, twiddle)
    smalls = [pltpu.make_async_copy(src, dst, small_s.at[i]) for i, (src, dst) in enumerate(zip(small, held))]
    for l in range(LEV):
        for i in range(3):
            load(i, l, cap0, CW, cs).start()
        if l == 0:
            smalls[2].start()
    for i, c in enumerate(smalls):
        if i != 2:
            c.start()
    for c in others:
        c.start()
    smalls[2].wait()

    lanes = lax.broadcasted_iota(jnp.int32, (C8, CW), 1)
    scap = cap_s[lat]
    row = lax.broadcasted_iota(jnp.int32, (WIN, 128), 0)
    lane1 = lanes[:SEG]
    pole = jnp.where(lat == 0, 0, CW - 1)

    @pl.loop(0, LEV)
    def _(l):
        for i in range(3):
            load(i, l, cap0, CW, cs).wait()
        fc = f[l, :, pl.ds(cap0, CW)]
        uc = u[l, :, pl.ds(cap0, CW)]
        vc = v[l, :, pl.ds(cap0, CW)]
        zero = jnp.zeros((1, CW), F32)
        e = jnp.concatenate([fc[1:], zero], axis=0)
        w = jnp.concatenate([zero, fc[:-1]], axis=0)
        n = jnp.where(jnp.logical_and(lane1 == pole, lat == 0), 0.0, pltpu.roll(fc, 1, 1))
        s = jnp.where(jnp.logical_and(lane1 == pole, lat == 1), 0.0, pltpu.roll(fc, CW - 1, 1))
        turn = lax.rem(CW - lat * SHIFT, CW)
        mm[0:SEG] = pltpu.roll(tend(fc, e, w, n, s, uc, vc, scap), turn, 1)
        mm[SEG : 2 * SEG] = pltpu.roll(uc, turn, 1)
        mm[2 * SEG : 3 * SEG] = pltpu.roll(vc, turn, 1)
        vt = mm[128 : 128 + TAIL]
        x12 = lax.rem(lanes[:WIN], 12)
        edge = pltpu.roll(fc, lax.rem(CW - lat * (SHIFT + 2) + 1, CW), 1)
        mx[0:SEG] = jnp.where(lane1 == jnp.where(lat == 0, 1, CAP + 2), edge, mm[0:SEG])
        for i in range(8):
            t0 = i + 1 if i < 7 else 15
            t15 = i + 8 if i < 7 else 0
            a0 = pltpu.roll(vt, CW - t0, 1)
            a15 = pltpu.roll(vt, 15 - t15, 1)
            mx[SEG + TAIL * i : SEG + TAIL * (i + 1)] = jnp.where(x12[:TAIL] == 3, a15, a0)
        ft = pltpu.roll(fc, turn, 1)
        f0 = jnp.broadcast_to(ft[0:1], (WIN, CW))
        f44 = jnp.broadcast_to(ft[SEG - 1 : SEG], (WIN, CW))
        f0 = pltpu.roll(f0, CW - 15, 1, stride=1, stride_axis=0)
        f44 = pltpu.roll(f44, 0, 1, stride=1, stride_axis=0)
        mx[COLS : COLS + WIN] = jnp.where(x12 == 3, f44, f0)
        mx[COLS + WIN : COLS + WIN + 1] = mm[SEG : SEG + 1]
        mx[COLS + WIN + 1 : COLS + WIN + 2] = mm[2 * SEG - 1 : 2 * SEG]
        for b in range(CW // 128):
            ln[128 * b : 128 * (b + 1)] = mm[0:128, 128 * b : 128 * (b + 1)].T
            lx[128 * b : 128 * (b + 1)] = mx[0:128, 128 * b : 128 * (b + 1)].T

        @pl.loop(0, PER // 8)
        def _(mo):
            for mi in range(4):
                m = 4 * mo + mi
                a = ln[pl.ds(pl.multiple_of(24 * m, 8), 32)]
                b = lx[pl.ds(pl.multiple_of(24 * m, 8), 32)]
                first = jnp.logical_and(m == 0, lat == 0)
                last = jnp.logical_and(m == PER // 2 - 1, lat == 1)
                use0 = jnp.logical_or(jnp.logical_and(row == 0, jnp.logical_not(first)), row == WIN - 1)
                use1 = jnp.logical_or(row == 0, jnp.logical_and(row == WIN - 1, jnp.logical_not(last)))
                msg[l * PER + 2 * m] = jnp.where(use0, b[0:16], a[0:16])
                msg[l * PER + 2 * m + 1] = jnp.where(use1, b[12:28], a[12:28])

        ext[l] = jnp.where(lat == 0, lx[0:2], lx[CAP + 2 : CAP + 4])

    pl.semaphore_wait(barrier, SEGS)

    def remote(src, dst, send, recv_sem, dev):
        return pltpu.make_async_remote_copy(
            src_ref=src, dst_ref=dst, send_sem=send, recv_sem=recv_sem,
            device_id=dev, device_id_type=MESH,
        )

    def send_line(d):
        return remote(msg.at[d], recv.at[lon], a_s, a_r, at(d))

    def spread(send):
        @pl.loop(0, (SEGS // 2 - 1) // 7)
        def _(k):
            for i in range(1, 8):
                send(lax.rem(lon + 7 * k + i, SEGS)).start()
                send(lax.rem(lon + SEGS - 7 * k - i, SEGS)).start()

        send(lax.rem(lon + SEGS // 2, SEGS)).start()

    def send_ext(l):
        d = l * PER + lat * (PER - 1)
        return d, remote(ext.at[l], ext_got.at[lon], x_s.at[l], x_r, at(d))

    for l in range(LEV):
        d, c = send_ext(l)

        @pl.when(d != lon)
        def _():
            c.start()

        @pl.when(d == lon)
        def _():
            ext_got[lon] = ext[l]

    spread(send_line)
    recv[lon] = msg[lon]

    for c in others:
        c.wait()
    for i, c in enumerate(smalls):
        if i != 2:
            c.wait()
    own = pl.multiple_of(lat * 128, 128)
    mid_w[...] = jnp.zeros_like(mid_w)
    mid_e[...] = jnp.zeros_like(mid_e)
    parts = ((fm, f, 0, 3), (um, u, 3, 2), (vm, v, 5, 2))
    for l in range(LEV):
        for ref, src, a, n in parts:
            mid_w[l, a : a + n] = src[l, 0:n, pl.ds(mid0, MW - 128)]
            mid_e[l, a : a + n] = src[l, SEG - n : SEG, pl.ds(mid0, MW - 128)]

    @pl.loop(0, LEV)
    def _(l):
        for ref, src, a, n in parts:
            ref[l, 3 : 3 + SEG, pl.ds(own, MW - 128)] = src[l, :, pl.ds(mid0, MW - 128)]

    mids = [
        remote(mid_w, mgot_e, ms.at[0], mr.at[0], west_dev),
        remote(mid_e, mgot_w, ms.at[1], mr.at[1], east_dev),
    ]
    src0 = pl.multiple_of((1 - lat) * (MW - 256) + lat * 128, 128)
    dst0 = pl.multiple_of(lat * (MW - 128), 128)
    lats = [
        remote(ref.at[:, :, pl.ds(src0, 128)], ref.at[:, :, pl.ds(dst0, 128)], ls.at[i], lr.at[i], partner)
        for i, ref in enumerate((fm, um, vm))
    ]

    def total(sem, ref, n):
        pltpu.make_async_copy(ref.at[pl.ds(0, n)], ref.at[pl.ds(0, n)], sem).wait()

    tt[:, SEG:C8] = jnp.zeros((WIN, C8 - SEG, 128), F32)
    uu[:, SEG:C8] = jnp.zeros((WIN, C8 - SEG, 128), F32)
    vv[:, SEG:C8] = jnp.zeros((WIN, C8 - SEG, 128), F32)
    sp[2] = jnp.zeros((128, 128), F32)

    @pl.when(jnp.logical_or(north_pole, south_pole))
    def _():
        total(x_r, ext_got, SEGS - 1)

    @pl.when(north_pole)
    def _():
        sp[3] = ext_got[:, 0, :].T
        sp[2] = ext_got[:, 1, :].T

    @pl.when(south_pole)
    def _():
        sp[3] = ext_got[:, 1, :].T
        sp[2] = ext_got[:, 0, :].T

    total(a_s, msg, SEGS - 1)
    for c in mids:
        c.start()
    total(a_r, recv, SEGS - 1)
    for t in range(WIN):
        w = recv[:, t, :].T
        tt[t, 0:SEG] = w[0:SEG]
        uu[t, 0:SEG] = (-0.05 * rows_s[lat, CHUNK * jj + t]) * w[SEG : 2 * SEG]
        vv[t, 0 : SEG - TAIL] = -0.05 * w[2 * SEG : 128]
        if t == 0:
            sp[0] = w
        if t == WIN - 1:
            sp[1] = w

    @pl.when(north_pole)
    def _():
        sp[0] = sp[3]

    @pl.when(south_pole)
    def _():
        sp[1] = sp[3]

    for i in range(8):
        t0 = i + 1 if i < 7 else 15
        t15 = i + 8 if i < 7 else 0
        lo, hi = SEG + TAIL * i, SEG + TAIL * (i + 1)
        vv[t0, SEG - TAIL : SEG] = -0.05 * sp[0, lo:hi]
        vv[t15, SEG - TAIL : SEG] = -0.05 * sp[1, lo:hi]

    e_in = pltpu.roll(sp[0, COLS - 5 : COLS + 19], 127, 1)
    w_in = pltpu.roll(sp[1, COLS - 5 : COLS + 19], 1, 1)
    for t in range(WIN):
        sw = rows_s[lat, CHUNK * jj + t]
        if t in (0, WIN - 1):
            u0 = (-0.05 * sw) * sp[t // (WIN - 1), COLS + WIN : COLS + WIN + 1]
            u44 = (-0.05 * sw) * sp[t // (WIN - 1), COLS + WIN + 1 : COLS + WIN + 2]
        else:
            u0, u44 = uu[t, 0:1], uu[t, SEG - 1 : SEG]
        r = 5 + 15 - t
        tt[t, SEG - 1 : SEG] += (0.02 * sw + u44) * e_in[r : r + 1]
        tt[t, 0:1] += (0.02 * sw - u0) * w_in[r : r + 1]
    opp = pltpu.roll(sp[2, 0:C8], SEGS // 2, 1)[:SEG]
    tt[0, 0:SEG] += jnp.where(north_pole, vv[0, 0:SEG] * opp, 0.0)
    tt[WIN - 1, 0:SEG] -= jnp.where(south_pole, vv[WIN - 1, 0:SEG] * opp, 0.0)

    col = lax.broadcasted_iota(jnp.int32, (C8, 128), 0)
    m_lane = lax.rem(lax.broadcasted_iota(jnp.int32, (1, KMAX), 1), KMAX // 2)
    o_lane = jnp.where(m_lane == 0, KMAX // 2, KMAX - m_lane)
    w_m = jnp.where(m_lane == 0, 1.0 / (SEG * SEGS), 2.0 / (SEG * SEGS))
    w_o = 2.0 / (SEG * SEGS)

    def lap(old, t):
        g = old[t]
        g8 = pltpu.roll(g[0:8], 127, 1)
        g40 = pltpu.roll(g[40:48], 1, 1)
        e = jnp.where(col == SEG - 1, jnp.broadcast_to(g8[0:1], (C8, 128)), pltpu.roll(g, C8 - 1, 0))
        w = jnp.where(col == 0, jnp.broadcast_to(g40[4:5], (C8, 128)), pltpu.roll(g, 1, 0))
        n = old[max(t - 1, 0)]
        s = old[min(t + 1, WIN - 1)]
        if t == 0:
            n = jnp.where(north_pole, pltpu.roll(g, SEGS // 2, 1), n)
        if t == WIN - 1:
            s = jnp.where(south_pole, pltpu.roll(g, SEGS // 2, 1), s)
        return uu[t] * (e - w) + vv[t] * (n - s) + (0.02 * rows_s[lat, CHUNK * jj + t]) * (e - 2.0 * g + w)

    def fold(z, table):
        p = jnp.sum(z * table, axis=0, keepdims=True)
        return p + pltpu.roll(p, KMAX // 2, 1)

    def substep(step, old, new, block):
        ts = range(BLOCK * block, BLOCK * (block + 1))
        raw = [tt[t] if step == 0 else tt[t] + lap(old, t) for t in ts]
        z = product(jnp.concatenate(raw, axis=0), fwd)
        modes = []
        for i, t in enumerate(ts):
            zt = z[C8 * i : C8 * (i + 1)]
            x = CHUNK * jj + t - 4 * lat
            cut = cuts[lat, jnp.minimum(jnp.maximum(x, 0), CAP - 1)]
            km = jnp.where(m_lane <= cut, w_m, 0.0)
            ko = jnp.where(o_lane <= cut, w_o, 0.0)
            modes.append(
                (fold(zt, twiddle[0]) * km) * twiddle[0]
                + (fold(zt, twiddle[1]) * km) * twiddle[1]
                + (fold(zt, twiddle[2]) * ko) * twiddle[2]
                + (fold(zt, twiddle[3]) * ko) * twiddle[3]
            )
        y = product(jnp.concatenate(modes, axis=0), inv)
        for i, t in enumerate(ts):
            x = CHUNK * jj + t - 4 * lat
            inside = jnp.logical_and(x >= 0, x < CAP)
            g = jnp.where(inside, y[C8 * i : C8 * (i + 1)], raw[i])
            new[t] = g if step == 0 else old[t] + g

    for step, (old, new) in enumerate(((gb, ga), (ga, gb), (gb, ga))):
        for block in range(WIN // BLOCK):
            substep(step, old, new, block)

    for i in range(CHUNK):
        st[SEG * i : SEG * (i + 1)] = ga[2 + i, 0:SEG]
    for i in range(2):
        st[SEG * (CHUNK + i) : SEG * (CHUNK + i + 1)] = jnp.where(lat == 0, ga[i, 0:SEG], ga[WIN - 2 + i, 0:SEG])
    st[SEG * (CHUNK + 2) :] = jnp.zeros((128 * RET - SEG * (CHUNK + 2), 128), F32)
    for p in range(RET):
        ret[:, p, :] = st[128 * p : 128 * (p + 1)].T

    def send_back(d):
        return remote(ret.at[d], back.at[lon], b_s, b_r.at[lon // PER], at(d))

    spread(send_back)
    back[lon] = ret[lon]
    for c in mids:
        c.wait()
    for l in range(LEV):
        for ref, src, a, n in parts:
            ref[l, 3 - n : 3, pl.ds(own, MW - 128)] = mgot_w[l, a : a + n]
            ref[l, 3 + SEG : 3 + SEG + n, pl.ds(own, MW - 128)] = mgot_e[l, a : a + n]
    for c in lats:
        c.start()

    for c in lats:
        c.wait()
    smid = mid_s[lat]

    @pl.loop(0, LEV)
    def _(l):
        for _ in range(3):
            x = fm[l]
            t = tend(
                x, pltpu.roll(x, 55, 0), pltpu.roll(x, 1, 0),
                pltpu.roll(x, 1, 1), pltpu.roll(x, MW - 1, 1), um[l], vm[l], smid,
            )
            fm[l] = x + t

    @pl.loop(0, LEV)
    def _(l):
        out[l, :, pl.ds(mid0, MW - 128)] = fm[l, 3 : 3 + SEG, pl.ds(own, MW - 128)]

    def store(l, first, lanes, half):
        return pltpu.make_async_copy(
            out.at[l, :, pl.ds(first, lanes)], out_hbm.at[:, l, pl.ds(first, lanes)], d_s.at[half, l]
        )

    stores = [store(l, rest0, ROWS - CW, 0) for l in range(LEV)]
    for c in stores:
        c.start()
    rl[:, CAP:CW] = jnp.zeros((LEV, CW - CAP, 128), F32)
    lane128 = lax.broadcasted_iota(jnp.int32, (PER, 128), 1)
    x = lane1 - lat * SHIFT
    inside = jnp.logical_and(x >= 2 * lat, x < CAP + 2 + 2 * lat)
    ends = []
    for order, step in enumerate((0, 1, 3, 2)):
        l = lax.rem(lon // PER + step, LEV)
        total(b_r.at[l], back, PER - 1 if order == 0 else PER)
        mine = back.at[pl.ds(pl.multiple_of(l * PER, PER), PER)]
        for i in range(CHUNK + 2):
            p, off = divmod(SEG * i, 128)
            r = mine[:, p, :]
            if off:
                r = pltpu.roll(r, 128 - off, 1)
            if off + SEG > 128:
                r = jnp.where(lane128 < 128 - off, r, pltpu.roll(mine[:, p + 1, :], 128 - off, 1))
            if i < CHUNK:
                rl[order, pl.ds(2 + i, PER, stride=CHUNK), :] = r
            else:
                rl[order, i - CHUNK : i - CHUNK + 1] = r[0:1]
                rl[order, CAP + 2 + i - CHUNK : CAP + 3 + i - CHUNK] = r[PER - 1 : PER]
        add = jnp.concatenate([rl[order, 128 * b : 128 * (b + 1)].T[0:C8] for b in range(CW // 128)], axis=1)
        add = pltpu.roll(add, lat * SHIFT, 1)[0:SEG]
        old = out[l, :, pl.ds(cap0, CW)]
        out[l, :, pl.ds(cap0, CW)] = jnp.where(inside, f[l, :, pl.ds(cap0, CW)] + add, old)
        ends.append(store(l, cap0, CW, 1))
        ends[-1].start()

    total(b_s, ret, SEGS - 1)
    for l in range(LEV):
        d, c = send_ext(l)

        @pl.when(d != lon)
        def _():
            c.wait_send()

    for c in stores + ends:
        c.wait()


def body(f, u, v, cutoffs):
    cap_s, mid_s, rows_s = stretch_table()
    small = (cutoffs, rows_s, cap_s, mid_s) + tables()
    V = lambda *shape: pltpu.VMEM(shape, F32)
    dma = pltpu.SemaphoreType.DMA
    f, u, v = (jnp.transpose(a, (1, 0, 2)) for a in (f, u, v))
    done = pl.pallas_call(
        kernel,
        out_shape=jax.ShapeDtypeStruct(f.shape, F32),
        in_specs=[pl.BlockSpec(memory_space=pl.ANY)] * (3 + SMALL),
        out_specs=pl.BlockSpec(memory_space=pl.ANY),
        scratch_shapes=[
            pltpu.SMEM(cutoffs.shape, jnp.int32), pltpu.SMEM(rows_s.shape, F32),
            V(*cap_s.shape), V(*mid_s.shape),
            pltpu.VMEM((256, 256), BF16), pltpu.VMEM((256, 256), BF16), V(4, C8, 128), dma((SMALL,)),
            V(LEV, SEG, ROWS), V(LEV, SEG, ROWS), V(LEV, SEG, ROWS), V(LEV, SEG, ROWS),
            V(LEV, 8, MW - 128), V(LEV, 8, MW - 128), V(LEV, 8, MW - 128), V(LEV, 8, MW - 128),
            V(LEV, 56, MW), V(LEV, 56, MW), V(LEV, 56, MW),
            V(136, CW), V(128, CW), V(CW, 128), V(CW, 128),
            V(SEGS, WIN, 128), V(SEGS, WIN, 128), V(LEV, 2, 128), V(SEGS, 2, 128), V(4, 128, 128),
            V(WIN, C8, 128), V(WIN, C8, 128), V(WIN, C8, 128), V(WIN, C8, 128), V(WIN, C8, 128),
            V(128 * RET, 128), V(SEGS, RET, 128), V(SEGS, RET, 128), V(LEV, CW, 128),
            dma((2, LEV)), dma((3, LEV)), dma((3, LEV)), dma((2,)), dma((2,)), dma((3,)), dma((3,)),
            dma, dma, dma((LEV,)), dma, dma, dma((LEV,)),
        ],
        compiler_params=pltpu.CompilerParams(
            collective_id=0, has_side_effects=True, vmem_limit_bytes=60 * 1024 * 1024
        ),
    )(f, u, v, *small)
    return jnp.transpose(done, (1, 0, 2))


def solution(mesh):
    placed = (P(None, "lon", "lat"), P(None, "lon", "lat"), P(None, "lon", "lat"), P())
    return jax.shard_map(
        body, mesh=mesh, in_specs=placed, out_specs=P(None, "lon", "lat"), check_vma=False
    )
```

```python
import functools
import math

import jax
import jax.numpy as jnp
import ml_dtypes
import numpy as np
from jax import lax
from jax.experimental import pallas as pl
from jax.experimental.pallas import tpu as pltpu
from jax.sharding import PartitionSpec as P

MESH = pl.DeviceIdType.MESH
LEV, SEG, ROWS, SEGS = 4, 45, 1152, 128
CAP = ROWS // 3
CHUNK, WIN = 12, 16
PER = CAP // CHUNK
CW = 512
SHIFT = CW - CAP - 4
MW = 1024
KMAX = 128
C8 = 48
BLOCK = 16
RET = 5
SMALL = 7
COLS = 101
TAIL = 7
F32, BF16 = jnp.float32, jnp.bfloat16


def split(x):
    hi = x.astype(ml_dtypes.bfloat16)
    return hi, (x - hi.astype(np.float32)).astype(ml_dtypes.bfloat16)


def two_parts(basis):
    hi, lo = split(np.ascontiguousarray(basis))
    return np.concatenate(
        [np.concatenate([hi, lo], axis=1), np.concatenate([hi, np.zeros_like(lo)], axis=1)], axis=0
    )


def tables():
    total = SEG * SEGS
    half = KMAX // 2
    m, s, c = np.arange(half), np.arange(SEGS), np.arange(SEG)
    a = 2 * np.pi * ((s[:, None] * m[None, :]) % SEGS) / SEGS
    sin = np.sin(a)
    sin[:, 0] = np.where(s % 2 == 0, 1.0, -1.0)
    basis = np.concatenate([np.cos(a), sin], axis=1).astype(np.float32)
    other = np.where(m == 0, half, KMAX - m)
    angle = lambda k: 2 * np.pi * (c[:, None] * k[None, :]) / total
    cm, sm, co, so = np.cos(angle(m)), np.sin(angle(m)), np.cos(angle(other)), np.sin(angle(other))
    ta, tb = np.concatenate([cm, -sm], axis=1), np.concatenate([sm, cm], axis=1)
    pa, pb = np.concatenate([co, so], axis=1), np.concatenate([so, -co], axis=1)
    ta[:, half], tb[:, half], pa[:, 0], pb[:, 0] = 0.0, 0.0, 0.0, 0.0
    pa[:, half], pb[:, half] = co[:, 0], so[:, 0]
    twiddle = np.pad(np.stack([ta, tb, pa, pb]), ((0, 0), (0, C8 - SEG), (0, 0))).astype(np.float32)
    return two_parts(basis), two_parts(basis.T), twiddle


def stretch_table():
    colat = np.float32(math.pi) * (np.arange(2 * ROWS).astype(np.float32) + np.float32(0.5))
    colat = (colat / np.float32(2 * ROWS)).astype(np.float32)
    s = np.float32(1.0) / np.maximum(np.sin(colat), np.float32(0.125))
    s = np.pad(s.astype(np.float32), (0, MW))
    cap = np.stack([s[:CW], s[2 * ROWS - CW : 2 * ROWS]])[:, None, :]
    mid = np.stack([s[256 : 256 + MW], s[ROWS - 128 : ROWS - 128 + MW]])[:, None, :]
    rows = np.stack([s[: CAP + 4], s[2 * ROWS - CAP - 4 : 2 * ROWS]])
    return cap, mid, rows


def tend(mid, east, west, north, south, u, v, s):
    return (
        -0.05 * s * u * (east - west)
        - 0.05 * v * (north - south)
        + 0.02 * s * (east - 2.0 * mid + west)
    )


def product(x, parts_ref):
    hi = x.astype(BF16)
    lo = (x - hi.astype(F32)).astype(BF16)
    r = jnp.dot(jnp.concatenate([hi, lo], axis=1), parts_ref[...], preferred_element_type=F32)
    return r[:, 0:128] + r[:, 128:]


def kernel(
    f_hbm, u_hbm, v_hbm, *rest,
):
    small, (out_hbm, *scratch) = rest[:SMALL], rest[SMALL:]
    run(f_hbm, u_hbm, v_hbm, small, out_hbm, *scratch)


def run(
    f_hbm, u_hbm, v_hbm, small, out_hbm,
    cuts, rows_s, cap_s, mid_s, fwd, inv, twiddle, small_s,
    out, f, u, v, mid_w, mid_e, mgot_w, mgot_e,
    fm, um, vm, mm, mx, ln, lx, msg, recv, ext, ext_got, sp,
    tt, uu, vv, ga, gb, st, ret, back, rl,
    d_s, cs, os, ms, mr, ls, lr, a_s, a_r, x_s, x_r, b_s, b_r,
):
    lat = lax.axis_index("lat")
    lon = lax.axis_index("lon")
    south = lat == 1
    jj = lax.rem(lon, PER)
    north_pole = jnp.logical_and(lat == 0, jj == 0)
    south_pole = jnp.logical_and(lat == 1, jj == PER - 1)
    at = lambda d: (lat, d)
    east_dev = at(lax.rem(lon + 1, SEGS))
    west_dev = at(lax.rem(lon + SEGS - 1, SEGS))
    partner = (1 - lat, lon)

    cap0 = pl.multiple_of(lat * (ROWS - CW), 128)
    mid0 = pl.multiple_of((1 - lat) * 256, 128)
    rest0 = pl.multiple_of((1 - lat) * CW, 128)
    pairs = ((f_hbm, f), (u_hbm, u), (v_hbm, v))

    def load(i, l, first, lanes, sems):
        src, dst = pairs[i]
        return pltpu.make_async_copy(
            src.at[:, l, pl.ds(first, lanes)], dst.at[l, :, pl.ds(first, lanes)], sems.at[i, l]
        )

    others = [load(i, l, rest0, ROWS - CW, os) for l in range(LEV) for i in range(3)]
    barrier = pltpu.get_barrier_semaphore()

    def greet(k):
        pl.semaphore_signal(barrier, inc=1, device_id=at(lax.rem(lon + k, SEGS)), device_id_type=MESH)

    greet(SEGS // 2)

    @pl.loop(0, (SEGS // 2 - 1) // 7)
    def _(k):
        for i in range(1, 8):
            greet(SEGS // 2 - 7 * k - i)
            greet(SEGS // 2 + 7 * k + i)

    pl.semaphore_signal(barrier, inc=1, device_id=partner, device_id_type=MESH)

    held = (cuts, rows_s, cap_s, mid_s, fwd, inv, twiddle)
    smalls = [pltpu.make_async_copy(src, dst, small_s.at[i]) for i, (src, dst) in enumerate(zip(small, held))]
    for l in range(LEV):
        for i in range(3):
            load(i, l, cap0, CW, cs).start()
        if l == 0:
            smalls[2].start()
    for i, c in enumerate(smalls):
        if i != 2:
            c.start()
    for c in others:
        c.start()
    smalls[2].wait()

    lanes = lax.broadcasted_iota(jnp.int32, (C8, CW), 1)
    scap = cap_s[lat]
    row = lax.broadcasted_iota(jnp.int32, (WIN, 128), 0)
    lane1 = lanes[:SEG]
    pole = jnp.where(lat == 0, 0, CW - 1)

    @pl.loop(0, LEV)
    def _(l):
        for i in range(3):
            load(i, l, cap0, CW, cs).wait()
        fc = f[l, :, pl.ds(cap0, CW)]
        uc = u[l, :, pl.ds(cap0, CW)]
        vc = v[l, :, pl.ds(cap0, CW)]
        zero = jnp.zeros((1, CW), F32)
        e = jnp.concatenate([fc[1:], zero], axis=0)
        w = jnp.concatenate([zero, fc[:-1]], axis=0)
        n = jnp.where(jnp.logical_and(lane1 == pole, lat == 0), 0.0, pltpu.roll(fc, 1, 1))
        s = jnp.where(jnp.logical_and(lane1 == pole, lat == 1), 0.0, pltpu.roll(fc, CW - 1, 1))
        turn = lax.rem(CW - lat * SHIFT, CW)
        mm[0:SEG] = pltpu.roll(tend(fc, e, w, n, s, uc, vc, scap), turn, 1)
        mm[SEG : 2 * SEG] = pltpu.roll(uc, turn, 1)
        mm[2 * SEG : 3 * SEG] = pltpu.roll(vc, turn, 1)
        vt = mm[128 : 128 + TAIL]
        x12 = lax.rem(lanes[:WIN], 12)
        edge = pltpu.roll(fc, lax.rem(CW - lat * (SHIFT + 2) + 1, CW), 1)
        mx[0:SEG] = jnp.where(lane1 == jnp.where(lat == 0, 1, CAP + 2), edge, mm[0:SEG])
        for i in range(8):
            t0 = i + 1 if i < 7 else 15
            t15 = i + 8 if i < 7 else 0
            a0 = pltpu.roll(vt, CW - t0, 1)
            a15 = pltpu.roll(vt, 15 - t15, 1)
            mx[SEG + TAIL * i : SEG + TAIL * (i + 1)] = jnp.where(x12[:TAIL] == 3, a15, a0)
        ft = pltpu.roll(fc, turn, 1)
        f0 = jnp.broadcast_to(ft[0:1], (WIN, CW))
        f44 = jnp.broadcast_to(ft[SEG - 1 : SEG], (WIN, CW))
        f0 = pltpu.roll(f0, CW - 15, 1, stride=1, stride_axis=0)
        f44 = pltpu.roll(f44, 0, 1, stride=1, stride_axis=0)
        mx[COLS : COLS + WIN] = jnp.where(x12 == 3, f44, f0)
        mx[COLS + WIN : COLS + WIN + 1] = mm[SEG : SEG + 1]
        mx[COLS + WIN + 1 : COLS + WIN + 2] = mm[2 * SEG - 1 : 2 * SEG]
        for b in range(CW // 128):
            ln[128 * b : 128 * (b + 1)] = mm[0:128, 128 * b : 128 * (b + 1)].T
            lx[128 * b : 128 * (b + 1)] = mx[0:128, 128 * b : 128 * (b + 1)].T

        @pl.loop(0, PER // 8)
        def _(mo):
            for mi in range(4):
                m = 4 * mo + mi
                a = ln[pl.ds(pl.multiple_of(24 * m, 8), 32)]
                b = lx[pl.ds(pl.multiple_of(24 * m, 8), 32)]
                first = jnp.logical_and(m == 0, lat == 0)
                last = jnp.logical_and(m == PER // 2 - 1, lat == 1)
                use0 = jnp.logical_or(jnp.logical_and(row == 0, jnp.logical_not(first)), row == WIN - 1)
                use1 = jnp.logical_or(row == 0, jnp.logical_and(row == WIN - 1, jnp.logical_not(last)))
                msg[l * PER + 2 * m] = jnp.where(use0, b[0:16], a[0:16])
                msg[l * PER + 2 * m + 1] = jnp.where(use1, b[12:28], a[12:28])

        ext[l] = jnp.where(lat == 0, lx[0:2], lx[CAP + 2 : CAP + 4])

    pl.semaphore_wait(barrier, SEGS)

    def remote(src, dst, send, recv_sem, dev):
        return pltpu.make_async_remote_copy(
            src_ref=src, dst_ref=dst, send_sem=send, recv_sem=recv_sem,
            device_id=dev, device_id_type=MESH,
        )

    def send_line(d):
        return remote(msg.at[d], recv.at[lon], a_s, a_r, at(d))

    def spread(send):
        @pl.loop(0, (SEGS // 2 - 1) // 7)
        def _(k):
            for i in range(1, 8):
                send(lax.rem(lon + 7 * k + i, SEGS)).start()
                send(lax.rem(lon + SEGS - 7 * k - i, SEGS)).start()

        send(lax.rem(lon + SEGS // 2, SEGS)).start()

    def send_ext(l):
        d = l * PER + lat * (PER - 1)
        return d, remote(ext.at[l], ext_got.at[lon], x_s.at[l], x_r, at(d))

    for l in range(LEV):
        d, c = send_ext(l)

        @pl.when(d != lon)
        def _():
            c.start()

        @pl.when(d == lon)
        def _():
            ext_got[lon] = ext[l]

    spread(send_line)
    recv[lon] = msg[lon]

    for c in others:
        c.wait()
    for i, c in enumerate(smalls):
        if i != 2:
            c.wait()
    own = pl.multiple_of(lat * 128, 128)
    mid_w[...] = jnp.zeros_like(mid_w)
    mid_e[...] = jnp.zeros_like(mid_e)
    parts = ((fm, f, 0, 3), (um, u, 3, 2), (vm, v, 5, 2))
    for l in range(LEV):
        for ref, src, a, n in parts:
            mid_w[l, a : a + n] = src[l, 0:n, pl.ds(mid0, MW - 128)]
            mid_e[l, a : a + n] = src[l, SEG - n : SEG, pl.ds(mid0, MW - 128)]

    @pl.loop(0, LEV)
    def _(l):
        for ref, src, a, n in parts:
            ref[l, 3 : 3 + SEG, pl.ds(own, MW - 128)] = src[l, :, pl.ds(mid0, MW - 128)]

    mids = [
        remote(mid_w, mgot_e, ms.at[0], mr.at[0], west_dev),
        remote(mid_e, mgot_w, ms.at[1], mr.at[1], east_dev),
    ]
    src0 = pl.multiple_of((1 - lat) * (MW - 256) + lat * 128, 128)
    dst0 = pl.multiple_of(lat * (MW - 128), 128)
    lats = [
        remote(ref.at[:, :, pl.ds(src0, 128)], ref.at[:, :, pl.ds(dst0, 128)], ls.at[i], lr.at[i], partner)
        for i, ref in enumerate((fm, um, vm))
    ]

    def total(sem, ref, n):
        pltpu.make_async_copy(ref.at[pl.ds(0, n)], ref.at[pl.ds(0, n)], sem).wait()

    total(a_s, msg, SEGS - 1)
    for c in mids:
        c.start()
    total(a_r, recv, SEGS - 1)
    tt[:, SEG:C8] = jnp.zeros((WIN, C8 - SEG, 128), F32)
    uu[:, SEG:C8] = jnp.zeros((WIN, C8 - SEG, 128), F32)
    vv[:, SEG:C8] = jnp.zeros((WIN, C8 - SEG, 128), F32)
    for t in range(WIN):
        w = recv[:, t, :].T
        tt[t, 0:SEG] = w[0:SEG]
        uu[t, 0:SEG] = w[SEG : 2 * SEG]
        vv[t, 0 : SEG - TAIL] = w[2 * SEG : 128]
        if t == 0:
            sp[0] = w
        if t == WIN - 1:
            sp[1] = w

    @pl.when(jnp.logical_or(north_pole, south_pole))
    def _():
        total(x_r, ext_got, SEGS - 1)

    sp[2] = jnp.zeros((128, 128), F32)

    @pl.when(north_pole)
    def _():
        sp[0] = ext_got[:, 0, :].T
        sp[2] = ext_got[:, 1, :].T

    @pl.when(south_pole)
    def _():
        sp[1] = ext_got[:, 1, :].T
        sp[2] = ext_got[:, 0, :].T

    for i in range(8):
        t0 = i + 1 if i < 7 else 15
        t15 = i + 8 if i < 7 else 0
        lo, hi = SEG + TAIL * i, SEG + TAIL * (i + 1)
        vv[t0, SEG - TAIL : SEG] = sp[0, lo:hi]
        vv[t15, SEG - TAIL : SEG] = sp[1, lo:hi]

    e_in = pltpu.roll(sp[0, COLS - 5 : COLS + 19], 127, 1)
    w_in = pltpu.roll(sp[1, COLS - 5 : COLS + 19], 1, 1)
    for t in range(WIN):
        sw = rows_s[lat, CHUNK * jj + t]
        if t in (0, WIN - 1):
            u0 = sp[t // (WIN - 1), COLS + WIN : COLS + WIN + 1]
            u44 = sp[t // (WIN - 1), COLS + WIN + 1 : COLS + WIN + 2]
        else:
            u0, u44 = uu[t, 0:1], uu[t, SEG - 1 : SEG]
        r = 5 + 15 - t
        tt[t, SEG - 1 : SEG] += (0.02 * sw - 0.05 * sw * u44) * e_in[r : r + 1]
        tt[t, 0:1] += (0.02 * sw + 0.05 * sw * u0) * w_in[r : r + 1]
    opp = 0.05 * pltpu.roll(sp[2, 0:C8], SEGS // 2, 1)[:SEG]
    tt[0, 0:SEG] -= jnp.where(north_pole, vv[0, 0:SEG] * opp, 0.0)
    tt[WIN - 1, 0:SEG] += jnp.where(south_pole, vv[WIN - 1, 0:SEG] * opp, 0.0)

    col = lax.broadcasted_iota(jnp.int32, (C8, 128), 0)
    m_lane = lax.rem(lax.broadcasted_iota(jnp.int32, (1, KMAX), 1), KMAX // 2)
    o_lane = jnp.where(m_lane == 0, KMAX // 2, KMAX - m_lane)
    w_m = jnp.where(m_lane == 0, 1.0 / (SEG * SEGS), 2.0 / (SEG * SEGS))
    w_o = 2.0 / (SEG * SEGS)

    def lap(old, t):
        g = old[t]
        g8 = pltpu.roll(g[0:8], 127, 1)
        g40 = pltpu.roll(g[40:48], 1, 1)
        e = jnp.where(col == SEG - 1, jnp.broadcast_to(g8[0:1], (C8, 128)), pltpu.roll(g, C8 - 1, 0))
        w = jnp.where(col == 0, jnp.broadcast_to(g40[4:5], (C8, 128)), pltpu.roll(g, 1, 0))
        n = old[max(t - 1, 0)]
        s = old[min(t + 1, WIN - 1)]
        if t == 0:
            n = jnp.where(north_pole, pltpu.roll(g, SEGS // 2, 1), n)
        if t == WIN - 1:
            s = jnp.where(south_pole, pltpu.roll(g, SEGS // 2, 1), s)
        return tend(g, e, w, n, s, uu[t], vv[t], rows_s[lat, CHUNK * jj + t])

    def fold(z, table):
        p = jnp.sum(z * table, axis=0, keepdims=True)
        return p + pltpu.roll(p, KMAX // 2, 1)

    def substep(step, old, new, block):
        ts = range(BLOCK * block, BLOCK * (block + 1))
        raw = [tt[t] if step == 0 else tt[t] + lap(old, t) for t in ts]
        z = product(jnp.concatenate(raw, axis=0), fwd)
        modes = []
        for i, t in enumerate(ts):
            zt = z[C8 * i : C8 * (i + 1)]
            x = CHUNK * jj + t - 4 * lat
            cut = cuts[lat, jnp.minimum(jnp.maximum(x, 0), CAP - 1)]
            km = jnp.where(m_lane <= cut, w_m, 0.0)
            ko = jnp.where(o_lane <= cut, w_o, 0.0)
            modes.append(
                (fold(zt, twiddle[0]) * km) * twiddle[0]
                + (fold(zt, twiddle[1]) * km) * twiddle[1]
                + (fold(zt, twiddle[2]) * ko) * twiddle[2]
                + (fold(zt, twiddle[3]) * ko) * twiddle[3]
            )
        y = product(jnp.concatenate(modes, axis=0), inv)
        for i, t in enumerate(ts):
            x = CHUNK * jj + t - 4 * lat
            inside = jnp.logical_and(x >= 0, x < CAP)
            g = jnp.where(inside, y[C8 * i : C8 * (i + 1)], raw[i])
            new[t] = g if step == 0 else old[t] + g

    for step, (old, new) in enumerate(((gb, ga), (ga, gb), (gb, ga))):
        for block in range(WIN // BLOCK):
            substep(step, old, new, block)

    for i in range(CHUNK):
        st[SEG * i : SEG * (i + 1)] = ga[2 + i, 0:SEG]
    for i in range(2):
        st[SEG * (CHUNK + i) : SEG * (CHUNK + i + 1)] = jnp.where(lat == 0, ga[i, 0:SEG], ga[WIN - 2 + i, 0:SEG])
    st[SEG * (CHUNK + 2) :] = jnp.zeros((128 * RET - SEG * (CHUNK + 2), 128), F32)
    for p in range(RET):
        ret[:, p, :] = st[128 * p : 128 * (p + 1)].T

    def send_back(d):
        return remote(ret.at[d], back.at[lon], b_s, b_r.at[lon // PER], at(d))

    spread(send_back)
    back[lon] = ret[lon]
    for c in mids:
        c.wait()
    for l in range(LEV):
        for ref, src, a, n in parts:
            ref[l, 3 - n : 3, pl.ds(own, MW - 128)] = mgot_w[l, a : a + n]
            ref[l, 3 + SEG : 3 + SEG + n, pl.ds(own, MW - 128)] = mgot_e[l, a : a + n]
    for c in lats:
        c.start()

    for c in lats:
        c.wait()
    smid = mid_s[lat]

    @pl.loop(0, LEV)
    def _(l):
        for _ in range(3):
            x = fm[l]
            t = tend(
                x, pltpu.roll(x, 55, 0), pltpu.roll(x, 1, 0),
                pltpu.roll(x, 1, 1), pltpu.roll(x, MW - 1, 1), um[l], vm[l], smid,
            )
            fm[l] = x + t

    @pl.loop(0, LEV)
    def _(l):
        out[l, :, pl.ds(mid0, MW - 128)] = fm[l, 3 : 3 + SEG, pl.ds(own, MW - 128)]

    def store(l, first, lanes, half):
        return pltpu.make_async_copy(
            out.at[l, :, pl.ds(first, lanes)], out_hbm.at[:, l, pl.ds(first, lanes)], d_s.at[half, l]
        )

    stores = [store(l, rest0, ROWS - CW, 0) for l in range(LEV)]
    for c in stores:
        c.start()
    rl[:, CAP:CW] = jnp.zeros((LEV, CW - CAP, 128), F32)
    lane128 = lax.broadcasted_iota(jnp.int32, (PER, 128), 1)
    x = lane1 - lat * SHIFT
    inside = jnp.logical_and(x >= 2 * lat, x < CAP + 2 + 2 * lat)
    ends = []
    for order, step in enumerate((0, 1, 3, 2)):
        l = lax.rem(lon // PER + step, LEV)
        total(b_r.at[l], back, PER - 1 if order == 0 else PER)
        mine = back.at[pl.ds(pl.multiple_of(l * PER, PER), PER)]
        for i in range(CHUNK + 2):
            p, off = divmod(SEG * i, 128)
            r = mine[:, p, :]
            if off:
                r = pltpu.roll(r, 128 - off, 1)
            if off + SEG > 128:
                r = jnp.where(lane128 < 128 - off, r, pltpu.roll(mine[:, p + 1, :], 128 - off, 1))
            if i < CHUNK:
                rl[order, pl.ds(2 + i, PER, stride=CHUNK), :] = r
            else:
                rl[order, i - CHUNK : i - CHUNK + 1] = r[0:1]
                rl[order, CAP + 2 + i - CHUNK : CAP + 3 + i - CHUNK] = r[PER - 1 : PER]
        add = jnp.concatenate([rl[order, 128 * b : 128 * (b + 1)].T[0:C8] for b in range(CW // 128)], axis=1)
        add = pltpu.roll(add, lat * SHIFT, 1)[0:SEG]
        old = out[l, :, pl.ds(cap0, CW)]
        out[l, :, pl.ds(cap0, CW)] = jnp.where(inside, f[l, :, pl.ds(cap0, CW)] + add, old)
        ends.append(store(l, cap0, CW, 1))
        ends[-1].start()

    total(b_s, ret, SEGS - 1)
    for l in range(LEV):
        d, c = send_ext(l)

        @pl.when(d != lon)
        def _():
            c.wait_send()

    for c in stores + ends:
        c.wait()


def body(f, u, v, cutoffs):
    cap_s, mid_s, rows_s = stretch_table()
    small = (cutoffs, rows_s, cap_s, mid_s) + tables()
    V = lambda *shape: pltpu.VMEM(shape, F32)
    dma = pltpu.SemaphoreType.DMA
    f, u, v = (jnp.transpose(a, (1, 0, 2)) for a in (f, u, v))
    done = pl.pallas_call(
        kernel,
        out_shape=jax.ShapeDtypeStruct(f.shape, F32),
        in_specs=[pl.BlockSpec(memory_space=pl.ANY)] * (3 + SMALL),
        out_specs=pl.BlockSpec(memory_space=pl.ANY),
        scratch_shapes=[
            pltpu.SMEM(cutoffs.shape, jnp.int32), pltpu.SMEM(rows_s.shape, F32),
            V(*cap_s.shape), V(*mid_s.shape),
            pltpu.VMEM((256, 256), BF16), pltpu.VMEM((256, 256), BF16), V(4, C8, 128), dma((SMALL,)),
            V(LEV, SEG, ROWS), V(LEV, SEG, ROWS), V(LEV, SEG, ROWS), V(LEV, SEG, ROWS),
            V(LEV, 8, MW - 128), V(LEV, 8, MW - 128), V(LEV, 8, MW - 128), V(LEV, 8, MW - 128),
            V(LEV, 56, MW), V(LEV, 56, MW), V(LEV, 56, MW),
            V(136, CW), V(128, CW), V(CW, 128), V(CW, 128),
            V(SEGS, WIN, 128), V(SEGS, WIN, 128), V(LEV, 2, 128), V(SEGS, 2, 128), V(3, 128, 128),
            V(WIN, C8, 128), V(WIN, C8, 128), V(WIN, C8, 128), V(WIN, C8, 128), V(WIN, C8, 128),
            V(128 * RET, 128), V(SEGS, RET, 128), V(SEGS, RET, 128), V(LEV, CW, 128),
            dma((2, LEV)), dma((3, LEV)), dma((3, LEV)), dma((2,)), dma((2,)), dma((3,)), dma((3,)),
            dma, dma, dma((LEV,)), dma, dma, dma((LEV,)),
        ],
        compiler_params=pltpu.CompilerParams(
            collective_id=0, has_side_effects=True, vmem_limit_bytes=60 * 1024 * 1024
        ),
    )(f, u, v, *small)
    return jnp.transpose(done, (1, 0, 2))


def solution(mesh):
    placed = (P(None, "lon", "lat"), P(None, "lon", "lat"), P(None, "lon", "lat"), P())
    return jax.shard_map(
        body, mesh=mesh, in_specs=placed, out_specs=P(None, "lon", "lat"), check_vma=False
    )
```
